32 devices in a mesh: depth: 4 (over y, x), row: 2 (over core), col: 4 (over z).
Axes of the slice: x: 2, y: 2, z: 4, core: 2. Of those that a mesh axis runs over, the one named last changes fastest.
Arguments:
- species: float32 [2, 64, 64, 512], P(None, 'depth', 'row', 'col'), may hold values from -6 to 6
- diffusivity: float32 [64, 64, 512], P('depth', 'row', 'col'), may hold values from 0.05 to 0.4
- reaction_rate: float32 [64, 64, 512], P('depth', 'row', 'col'), may hold values from 0.2 to 2
- shear_rate: float32 [16], replicated, may hold values from -0.08 to 0.08
- colour_weight: float32 [16, 4, 2], replicated, may hold values from -4 to 4
- colour_bias: float32 [16, 4], replicated, may hold values from -1 to 1
- slab_order: int32 [16, 4], replicated, may hold values from 0 to 3, each once within a row
- lengths: int32 [16, 4, 64], P('depth', 'col', 'row'), may hold values from 1 to 128
- owners: int32 [16, 4, 64, 1], P('depth', 'col', 'row'), may hold values from 0 to 3; in each aligned block of 32 rows (0 to 31, 32 to 63, ..., all dimensions but the last counted through in order) at most 16 rows name the same one
- warp_matrix: bfloat16 [16, 128, 128], replicated, may hold values from -0.5 to 0.5
Outputs:
- species_out: float32 [2, 64, 64, 512], P(None, 'depth', 'row', 'col')
- frame: float32 [16, 64, 4, 512], P('depth', 'row', None, 'col')
The draws below stay inside these ranges and needn't reach their ends.
Inputs may be any that keep to these rules, and one draw needn't show every extreme that they name: `slab_order`: each row names each of the 4 slabs once. `owners`: for one view, the 32 scanlines of one device (aligned blocks of 32 along the third dimension) name any one owner at most 16 times.
All inputs are finite; a program needn't handle non-finite values.
Results may differ from the reference program's by a relative error of at most 0.001.
The reference program's roundings to bfloat16 on the way (of `picture` and `pieces`) count: a program that leaves them out, or rounds other values in their place, can miss the bound.
Values may be sent and summed in bfloat16 or wider, within the bound.
A program may use at most 64 MiB of HBM per device.

```python
import math
import jax
import jax.numpy as jnp
import numpy as np
from jax import lax

CD = 16
CR = 32
CC = 128
VIEWS = 16
NDZ = 64
NR = 64
NC = 512
NSLAB = 4
NTILE = 4
SH = 3
CAP = 16


def draw_lengths(key, part):
    values = jax.random.randint(key, (VIEWS, NTILE, NR), 1, CC + 1, dtype=jnp.int32)
    values = values.at[0, 0, 0].set(CC)
    return values.at[0, 0, 1].set(1)


def steps_of(own_key, extent, shards, least, top_value):
    gain, own = 1.0, jax.random.fold_in(own_key, 6)
    for axis_at, shards_of in shards:
        draws = jnp.exp(jax.random.uniform(jax.random.fold_in(own, axis_at), (shards_of,), jnp.float32, least / len(shards), top_value / len(shards)))
        gain = gain * jnp.repeat(draws, extent[axis_at] // shards_of).reshape([-1 if axis == axis_at else 1 for axis in range(len(extent))])
    return gain


def deal_out(rng, own, number, rows, count, top, bound, lean):
    sequence = jax.random.permutation(rng, count)
    heavy_load, usual = portions_of(count, rows * top, bound, lean, True), portions_of(count, rows * top, bound, lean, False)
    places = jnp.arange(count)

    def named(sizes, rotation):
        used = int((sizes > 0).sum())
        fixed = max(1, used // 4)
        passed = fixed + (places - fixed + rotation * (used - fixed)) % max(1, count - fixed)
        return jnp.zeros((count,), jnp.int32).at[sequence[jnp.where(places < fixed, places, passed)]].set(jnp.asarray(sizes, jnp.int32))

    sizes = jnp.where(number % 4 == 0, named(heavy_load, number // 4), named(usual, number - number // 4 - 1))
    mixed = jax.random.permutation(jax.random.fold_in(own, 3), count)
    source_of, taker = mixed[0:count // 2 * 2:2], mixed[1:count // 2 * 2:2]
    room = jnp.minimum(sizes[source_of] - 1, bound - sizes[taker]) // 2
    room = jnp.where((source_of == sequence[0]) | (taker == sequence[0]) | (sizes[taker] == 0), 0, jnp.maximum(room, 0))
    passed = jax.random.randint(jax.random.fold_in(own, 4), (count // 2,), 0, 1 << 20) % (room + 1)
    sizes = sizes.at[source_of].add(-passed).at[taker].add(passed)
    labels = jnp.searchsorted(jnp.cumsum(sizes), jnp.arange(rows * top), side="right").astype(jnp.int32)
    listing = labels.reshape(top, rows).T
    listing = listing[jax.random.permutation(jax.random.fold_in(own, 1), rows)]
    rotation = jax.random.randint(jax.random.fold_in(own, 2), (rows, 1), 0, top)
    return jnp.take_along_axis(listing, (jnp.arange(top)[None, :] + rotation) % top, axis=1)


def portions_of(number_of, total, bound, slope, full):
    weights = [(1 << 20) // math.isqrt(standing ** slope) + 1 for standing in range(1, number_of + 1)]
    largest = bound if full else min(bound, max(-(-total // number_of), total * weights[0] // sum(weights)))
    least = 1 if total - largest >= number_of - 1 else 0
    counts, rest = [largest] + [least] * (number_of - 1), total - largest - least * (number_of - 1)
    while rest > 0:
        candidates = [i for i in range(1, number_of) if counts[i] < largest] or [i for i in range(1, number_of) if counts[i] < bound]
        pool, left = sum([weights[i] for i in candidates]), rest
        for i in candidates:
            more = min(bound - counts[i], max(1, left * weights[i] // pool), rest)
            counts[i] = counts[i] + more
            rest = rest - more
    return np.array(counts)


def scatter_about(key, shape, scale, bound, shards=(), held_as=jnp.bfloat16):
    drawn = scale * jax.random.normal(key, shape, jnp.float32)
    if shards:
        drawn = drawn * steps_of(key, shape, shards, -0.22, 0.18)
    return jnp.clip(drawn, -bound, bound).astype(held_as)


def setup_inputs(seed: int = 0) -> dict:
    keys = jax.random.split(jax.random.key(seed), 11)
    species = scatter_about(keys[0], (2, NDZ, NR, NC), 1.0, 6.0, ((1, 4), (2, 2), (3, 4)), jnp.float32)
    diffusivity = jnp.clip(jnp.exp(math.log(0.4) - 2.0794415 * jax.random.uniform(keys[1], (NDZ, NR, NC), jnp.float32) ** steps_of(keys[1], (NDZ, NR, NC), ((0, 4), (1, 2), (2, 4)), -0.2, 0.2)), 0.05, 0.4)
    reaction_rate = jnp.clip(jnp.exp(math.log(2.0) - 2.3025851 * jax.random.uniform(keys[2], (NDZ, NR, NC), jnp.float32) ** steps_of(keys[2], (NDZ, NR, NC), ((0, 4), (1, 2), (2, 4)), -0.2, 0.2)), 0.2, 2.0)
    shear_rate = jnp.clip(jax.random.uniform(keys[3], (VIEWS,), jnp.float32, -0.08, 0.08), -0.08, 0.08)
    colour_weight = scatter_about(keys[4], (VIEWS, 4, 2), 1.0, 4.0, (), jnp.float32)
    colour_bias = jnp.clip(jax.random.uniform(keys[5], (VIEWS, 4), jnp.float32, -1.0, 1.0), -1.0, 1.0)
    slab_order = jax.vmap(lambda own: jax.random.permutation(own, NSLAB))(jax.random.split(keys[6], VIEWS)).reshape((VIEWS, NSLAB)).astype(jnp.int32)
    lengths = draw_lengths(jax.random.fold_in(keys[10], 71), 0)
    owners_keys = jax.random.split(jax.random.fold_in(keys[8], 1), VIEWS * NTILE * NR // CR)
    owners_turns = jax.random.permutation(jax.random.fold_in(keys[8], 3), VIEWS * NTILE * NR // CR)
    owners = jax.vmap(lambda own, number: deal_out(jax.random.fold_in(keys[8], 2), own, number, CR, NTILE, 1, CAP, 2))(owners_keys, owners_turns).reshape((VIEWS, NTILE, NR, 1))
    warp_matrix = scatter_about(keys[9], (VIEWS, CC, CC), CC ** -0.5, 0.5)
    return {"species": species, "diffusivity": diffusivity, "reaction_rate": reaction_rate, "shear_rate": shear_rate, "colour_weight": colour_weight, "colour_bias": colour_bias, "slab_order": slab_order, "lengths": lengths, "owners": owners, "warp_matrix": warp_matrix}


TIME_STEP = 0.1
RAY_STEP = 0.02
VEL_DEPTH = 0.3
VEL_ROW = 0.2
VEL_COL = 0.4


def tendency_of(padded, diffusivity, reaction_rate):
    centre = padded[:, 1:-1, 1:-1, 1:-1]
    below_depth = padded[:, :-2, 1:-1, 1:-1]
    above_depth = padded[:, 2:, 1:-1, 1:-1]
    below_row = padded[:, 1:-1, :-2, 1:-1]
    above_row = padded[:, 1:-1, 2:, 1:-1]
    below_col = padded[:, 1:-1, 1:-1, :-2]
    above_col = padded[:, 1:-1, 1:-1, 2:]
    laplace = below_depth + above_depth + below_row + above_row + below_col + above_col - 6.0 * centre
    advect = VEL_DEPTH * (centre - below_depth) + VEL_ROW * (centre - below_row) + VEL_COL * (centre - below_col)
    heat_part = centre[1]
    burned = reaction_rate * centre[0] * heat_part * heat_part / (1.0 + heat_part * heat_part)
    source = jnp.stack([-burned, burned])
    return diffusivity * laplace - advect + source


def pad_fields(fields):
    return jnp.pad(fields, ((0, 0), (1, 1), (1, 1), (1, 1)))


def advance(species, diffusivity, reaction_rate):
    first = species + TIME_STEP * tendency_of(pad_fields(species), diffusivity, reaction_rate)
    second = 0.75 * species + 0.25 * (first + TIME_STEP * tendency_of(pad_fields(first), diffusivity, reaction_rate))
    return species / 3.0 + (2.0 / 3.0) * (second + TIME_STEP * tendency_of(pad_fields(second), diffusivity, reaction_rate))


def transfer(samples, weight_one, bias_one):
    logits = weight_one[None, :, 0, None] * samples[0][:, None, :] + weight_one[None, :, 1, None] * samples[1][:, None, :] + bias_one[None, :, None]
    colours = jax.nn.sigmoid(logits[:, :3, :])
    fading = jnp.exp(-RAY_STEP * jax.nn.softplus(logits[:, 3, :]))
    return colours, fading


def render_view(padded, shear_one, weight_one, bias_one, order_row):
    def march(state_pair, depth_index):
        colour, through = state_pair
        offset = shear_one * (depth_index.astype(jnp.float32) + 0.5 - 0.5 * NDZ)
        floor_part = jnp.floor(offset)
        fraction = offset - floor_part
        start = floor_part.astype(jnp.int32) + SH
        depth_plane = lax.dynamic_index_in_dim(padded, depth_index, 1, keepdims=False)
        left_sample = lax.dynamic_slice_in_dim(depth_plane, start, NC, 2)
        right_sample = lax.dynamic_slice_in_dim(depth_plane, start + 1, NC, 2)
        samples = (1.0 - fraction) * left_sample + fraction * right_sample
        colours, fading = transfer(samples, weight_one, bias_one)
        colour = colour + (through * (1.0 - fading))[:, None, :] * colours
        return (colour, through * fading), None

    images = []
    for slab in range(NSLAB):
        start_state = (jnp.zeros((NR, 3, NC), jnp.float32), jnp.ones((NR, NC), jnp.float32))
        indices = jnp.arange(slab * CD, (slab + 1) * CD, dtype=jnp.int32)
        (colour, through), unused = lax.scan(march, start_state, indices)
        images.append(jnp.concatenate([colour, (1.0 - through)[:, None, :]], axis=1))
    stack = jnp.stack(images)
    result = stack[order_row[0]]
    for position in range(1, NSLAB):
        result = result + (1.0 - result[:, 3:4, :]) * stack[order_row[position]]
    return result.astype(jnp.bfloat16)


def reference(species, diffusivity, reaction_rate, shear_rate, colour_weight, colour_bias, slab_order, lengths, owners, warp_matrix):
    species_out = advance(species, diffusivity, reaction_rate)
    padded = jnp.pad(species_out, ((0, 0), (0, 0), (0, 0), (SH, SH)))

    def one_view(inputs):
        shear_one, weight_one, bias_one, order_row = inputs
        return render_view(padded, shear_one, weight_one, bias_one, order_row)

    picture = lax.map(one_view, (shear_rate, colour_weight, colour_bias, slab_order))
    tiles = picture.reshape(VIEWS, NR, 4, NTILE, CC)
    column = jnp.arange(CC, dtype=jnp.int32)
    keep = column[None, None, None, :] < jnp.transpose(lengths, (0, 2, 1))[:, :, :, None]
    pieces = jnp.where(keep[:, :, None, :, :], tiles, jnp.zeros((), jnp.bfloat16))
    warped = jnp.einsum('vyctx,vxz->vyctz', pieces.astype(jnp.float32), warp_matrix.astype(jnp.float32), precision=lax.Precision.HIGHEST)
    tile_ids = jnp.arange(NTILE, dtype=jnp.int32)
    chosen = (owners[:, :, :, 0][:, :, :, None] == tile_ids).astype(jnp.float32)
    frame = jnp.einsum('vtyo,vyctz->vycoz', chosen, warped, precision=lax.Precision.HIGHEST)
    return species_out, frame.reshape(VIEWS, NR, 4, NC)
```

```python
import functools

import jax
import jax.numpy as jnp
from jax import lax
from jax.experimental import pallas as pl
from jax.experimental.pallas import tpu as pltpu
from jax.sharding import PartitionSpec as P

TIME_STEP = 0.1
RAY_STEP = 0.02
VEL_DEPTH = 0.3
VEL_ROW = 0.2
VEL_COL = 0.4


def with_halo(cells, sides, width):
    for axis, dim in sides:
        count = lax.axis_size(axis)
        ends = count - 1
        head = lax.slice_in_dim(cells, 0, width, axis=dim)
        tail = lax.slice_in_dim(cells, cells.shape[dim] - width, cells.shape[dim], axis=dim)
        cells = jnp.concatenate(
            [
                lax.ppermute(tail, axis, [(i, (i + 1) % count) for i in range(ends)]),
                cells,
                lax.ppermute(head, axis, [((i + 1) % count, i) for i in range(ends)]),
            ],
            axis=dim,
        )
    return cells


def tendency_of(padded, diffusivity, reaction_rate):
    centre = padded[:, 1:-1, 1:-1, 1:-1]
    below_depth = padded[:, :-2, 1:-1, 1:-1]
    above_depth = padded[:, 2:, 1:-1, 1:-1]
    below_row = padded[:, 1:-1, :-2, 1:-1]
    above_row = padded[:, 1:-1, 2:, 1:-1]
    below_col = padded[:, 1:-1, 1:-1, :-2]
    above_col = padded[:, 1:-1, 1:-1, 2:]
    laplace = (
        below_depth + above_depth + below_row + above_row + below_col + above_col - 6.0 * centre
    )
    advect = (
        VEL_DEPTH * (centre - below_depth)
        + VEL_ROW * (centre - below_row)
        + VEL_COL * (centre - below_col)
    )
    heat_part = centre[1]
    burned = reaction_rate * centre[0] * heat_part * heat_part / (1.0 + heat_part * heat_part)
    source = jnp.stack([-burned, burned])
    return diffusivity * laplace - advect + source


def trimmed(array, layers):
    depth_len = array.shape[-3]
    row_len = array.shape[-2]
    col_len = array.shape[-1]
    return array[
        ..., layers : depth_len - layers, layers : row_len - layers, layers : col_len - layers
    ]


def inside_grid(first_index, count, margin, total):
    places = first_index - margin + jnp.arange(count + 2 * margin, dtype=jnp.int32)
    return (places >= 0) & (places < total)


def advance_deep(species, diffusivity, reaction_rate, rim_width):
    depth_cells = species.shape[1]
    rows = species.shape[2]
    width = species.shape[3]
    packed = jnp.concatenate([species, diffusivity[None], reaction_rate[None]], axis=0)
    wide = with_halo(packed, (("col", 3),), 3 + rim_width)
    deep = with_halo(wide, (("depth", 1), ("row", 2)), 3)
    depth_ok = inside_grid(
        lax.axis_index("depth") * depth_cells, depth_cells, 3, depth_cells * lax.axis_size("depth")
    )
    row_ok = inside_grid(lax.axis_index("row") * rows, rows, 3, rows * lax.axis_size("row"))
    col_ok = inside_grid(
        lax.axis_index("col") * width, width, 3 + rim_width, width * lax.axis_size("col")
    )
    inside = depth_ok[:, None, None] & row_ok[None, :, None] & col_ok[None, None, :]
    fields = deep[:2]
    spread = deep[2]
    rates = deep[3]
    zero = jnp.zeros((), jnp.float32)
    first = trimmed(fields, 1) + TIME_STEP * tendency_of(
        fields, trimmed(spread, 1), trimmed(rates, 1)
    )
    first = jnp.where(trimmed(inside, 1)[None], first, zero)
    second = 0.75 * trimmed(fields, 2) + 0.25 * (
        trimmed(first, 1) + TIME_STEP * tendency_of(first, trimmed(spread, 2), trimmed(rates, 2))
    )
    second = jnp.where(trimmed(inside, 2)[None], second, zero)
    final = trimmed(fields, 3) / 3.0 + 2.0 / 3.0 * (
        trimmed(second, 1) + TIME_STEP * tendency_of(second, trimmed(spread, 3), trimmed(rates, 3))
    )
    final = jnp.where(trimmed(inside, 3)[None], final, zero)
    return final


MESH = pl.DeviceIdType.MESH


def march_kernel(
    depth_devices, tiles, capacity,
    start_ref, fraction_ref, weight_ref, bias_ref, order_ref,
    rimmed_ref, length_ref, key_by_channel_ref, key_by_row_ref, warp_ref,
    frame_ref,
    shifted, *scratch,
):
    view_count = frame_ref.shape[0]
    stacks = scratch[:view_count]
    images = scratch[view_count : 2 * view_count]
    packs = scratch[2 * view_count : 3 * view_count]
    arrivals = scratch[3 * view_count : 4 * view_count]
    keys, slab_send, slab_recv, tile_send, tile_recv, key_send, key_recv = scratch[4 * view_count :]
    depth_cells, rows, width = shifted.shape[0], shifted.shape[3], shifted.shape[4]
    shifts = shifted.shape[1]
    me_d, me_r, me_c = lax.axis_index("depth"), lax.axis_index("row"), lax.axis_index("col")

    def slab_of(step):
        return lax.rem(me_d + step, depth_devices)

    def tile_of(step):
        return lax.rem(me_c + step, tiles)

    barrier = pltpu.get_barrier_semaphore()
    for step in range(1, depth_devices):
        pl.semaphore_signal(barrier, inc=1, device_id=(slab_of(step), me_r, me_c), device_id_type=MESH)
    for step in range(1, tiles):
        pl.semaphore_signal(barrier, inc=1, device_id=(me_d, me_r, tile_of(step)), device_id_type=MESH)

    def shift_planes(cell, carry):
        for field in range(2):
            plane = rimmed_ref[field, cell]
            for shift in range(shifts):
                here = plane[:, shift : shift + width]
                shifted[cell, shift, 2 * field] = here
                shifted[cell, shift, 2 * field + 1] = plane[:, shift + 1 : shift + 1 + width] - here
        return carry

    lax.fori_loop(0, depth_cells, shift_planes, 0)
    pl.semaphore_wait(barrier, depth_devices - 1 + tiles - 1)

    key_copies = []
    for step in range(1, tiles):
        copy = pltpu.make_async_remote_copy(
            src_ref=key_by_row_ref, dst_ref=keys.at[me_c],
            send_sem=key_send.at[step], recv_sem=key_recv.at[step],
            device_id=(me_d, me_r, tile_of(step)), device_id_type=MESH,
        )
        copy.start()
        key_copies.append(copy)
    keys[me_c] = key_by_row_ref[...]

    def render(view, out_ref):
        weights = [[weight_ref[view, c, f] for f in range(2)] for c in range(4)]
        biases = [bias_ref[view, c] for c in range(4)]

        def cells(cell, state):
            red, green, blue, through = state
            at = start_ref[view, cell]
            fraction = fraction_ref[view, cell]
            s0 = shifted[cell, at, 0] + fraction * shifted[cell, at, 1]
            s1 = shifted[cell, at, 2] + fraction * shifted[cell, at, 3]
            logits = [weights[c][0] * s0 + weights[c][1] * s1 + biases[c] for c in range(4)]
            fading = jnp.exp(-RAY_STEP * jnp.log(1.0 + jnp.exp(logits[3])))
            later = through * fading
            share = through - later
            return (
                red + share * jnp.tanh(logits[0]),
                green + share * jnp.tanh(logits[1]),
                blue + share * jnp.tanh(logits[2]),
                later,
            )

        zero = jnp.zeros((rows, width), jnp.float32)
        red, green, blue, through = lax.fori_loop(
            0, depth_cells, cells, (zero, zero, zero, zero + 1.0), unroll=4
        )
        opacity = 1.0 - through
        out_ref[0] = 0.5 * (red + opacity)
        out_ref[1] = 0.5 * (green + opacity)
        out_ref[2] = 0.5 * (blue + opacity)
        out_ref[3] = opacity

    slots = 4 * capacity

    def render_group(number):
        copies = []
        for step in list(range(1, depth_devices)) + [0]:
            view = slab_of(step) * view_count + number
            if step == 0:
                render(view, stacks[number].at[me_d])
            else:
                render(view, images[number].at[step])
                copy = pltpu.make_async_remote_copy(
                    src_ref=images[number].at[step], dst_ref=stacks[number].at[me_d],
                    send_sem=slab_send.at[number, step], recv_sem=slab_recv.at[number, step],
                    device_id=(slab_of(step), me_r, me_c), device_id_type=MESH,
                )
                copy.start()
                copies.append(copy)
        return copies

    def composite(number):
        view = me_d * view_count + number
        stack = stacks[number]
        result = stack[order_ref[view, 0]]
        for position in range(1, depth_devices):
            result = result + (1.0 - result[3:4]) * stack[order_ref[view, position]]
        keep = lax.broadcasted_iota(jnp.int32, (rows, width), 1) < length_ref[number]
        picture = jnp.where(keep[None], result, 0.0).reshape(4 * rows, width).astype(jnp.bfloat16)
        line = lax.broadcasted_iota(jnp.int32, (tiles * slots, 4 * rows), 0)
        pixel = lax.broadcasted_iota(jnp.int32, (tiles * slots, 4 * rows), 1)
        wanted = (line // slots) * capacity + line % capacity
        key = key_by_channel_ref[number : number + 1, :]
        chosen = (wanted == key) & ((line // capacity) % 4 == pixel // rows)
        packed = jnp.dot(
            jnp.where(chosen, 1.0, 0.0).astype(jnp.bfloat16), picture, preferred_element_type=jnp.float32
        ).astype(jnp.bfloat16)
        packs[number][...] = packed.reshape(tiles, slots, width)
        arrivals[number][me_c] = packs[number][me_c]
        copies = []
        for step in range(1, tiles):
            copy = pltpu.make_async_remote_copy(
                src_ref=packs[number].at[tile_of(step)], dst_ref=arrivals[number].at[me_c],
                send_sem=tile_send.at[number, step], recv_sem=tile_recv.at[number, step],
                device_id=(me_d, me_r, tile_of(step)), device_id_type=MESH,
            )
            copy.start()
            copies.append(copy)
        return copies

    def warp(number):
        line = lax.broadcasted_iota(jnp.int32, (slots, 4 * rows), 0)
        pixel = lax.broadcasted_iota(jnp.int32, (slots, 4 * rows), 1)
        wanted = me_c * capacity + line % capacity
        same = line // capacity == pixel % 4
        places = [
            jnp.where((wanted == keys[tile, number : number + 1, :]) & same, 1.0, 0.0).astype(jnp.bfloat16)
            for tile in range(tiles)
        ]
        gathered = lax.dot_general(
            jnp.concatenate(places, axis=0),
            arrivals[number][...].reshape(tiles * slots, width),
            (((0,), (0,)), ((), ())),
            preferred_element_type=jnp.float32,
        )
        high = gathered.astype(jnp.bfloat16)
        low = (gathered - high.astype(jnp.float32)).astype(jnp.bfloat16)
        matrix = warp_ref[me_d * view_count + number]
        frame_ref[number] = jnp.dot(high, matrix, preferred_element_type=jnp.float32) + jnp.dot(
            low, matrix, preferred_element_type=jnp.float32
        )

    slab_copies, tile_copies = [], []
    for number in range(view_count):
        slab_copies.append(render_group(number))
        if number > 0:
            for copy in slab_copies[number - 1]:
                copy.wait()
            tile_copies.append(composite(number - 1))
    for copy in slab_copies[-1]:
        copy.wait()
    tile_copies.append(composite(view_count - 1))
    for copy in key_copies:
        copy.wait()
    for number in range(view_count):
        for copy in tile_copies[number]:
            copy.wait()
        warp(number)


def slot_keys(owner_rows, capacity):
    rows = owner_rows.shape[-1]
    same = owner_rows[..., :, None] == owner_rows[..., None, :]
    places = jnp.arange(rows, dtype=jnp.int32)
    rank = jnp.sum((same & (places[:, None] < places[None, :])).astype(jnp.int32), axis=-2)
    return owner_rows * capacity + rank


def body(
    species, diffusivity, reaction_rate, shear_rate, colour_weight, colour_bias,
    slab_order, lengths, owners, warp_matrix,
):
    depth_cells, rows, width = species.shape[1:]
    depth_devices = lax.axis_size("depth")
    tiles = lax.axis_size("col")
    depth_total = depth_cells * depth_devices
    rim_width = (4 * depth_total + 99) // 100
    rimmed = advance_deep(species, diffusivity, reaction_rate, rim_width)
    species_out = rimmed[:, :, :, rim_width : rim_width + width]
    views = shear_rate.shape[0]
    view_count = views // depth_devices
    capacity = 2 * rows // tiles
    cell_at = lax.axis_index("depth") * depth_cells + jnp.arange(depth_cells, dtype=jnp.int32)
    offset = shear_rate[:, None] * (cell_at.astype(jnp.float32) + 0.5 - 0.5 * depth_total)
    floor_part = jnp.floor(offset)
    fraction = offset - floor_part
    start = jnp.clip(floor_part.astype(jnp.int32) + rim_width, 0, 2 * rim_width - 1)
    halves = jnp.array([0.5, 0.5, 0.5, 1.0], jnp.float32)
    key = slot_keys(owners[:, 0, :, 0], capacity)
    key_by_channel = jnp.tile(key, (1, 4))
    key_by_row = jnp.repeat(key, 4, axis=1)
    slots = 4 * capacity
    vmem = pl.BlockSpec(memory_space=pltpu.VMEM)
    smem = pl.BlockSpec(memory_space=pltpu.SMEM)
    frame = pl.pallas_call(
        functools.partial(march_kernel, depth_devices, tiles, capacity),
        out_shape=jax.ShapeDtypeStruct((view_count, 4 * rows, width), jnp.float32),
        in_specs=[smem] * 5 + [vmem] * 5,
        out_specs=vmem,
        scratch_shapes=[pltpu.VMEM((depth_cells, 2 * rim_width, 4, rows, width), jnp.float32)]
        + [pltpu.VMEM((depth_devices, 4, rows, width), jnp.float32)] * view_count
        + [pltpu.VMEM((depth_devices, 4, rows, width), jnp.float32)] * view_count
        + [pltpu.VMEM((tiles, slots, width), jnp.bfloat16)] * view_count
        + [pltpu.VMEM((tiles, slots, width), jnp.bfloat16)] * view_count
        + [
            pltpu.VMEM((tiles, view_count, 4 * rows), jnp.int32),
            pltpu.SemaphoreType.DMA((view_count, depth_devices)),
            pltpu.SemaphoreType.DMA((view_count, depth_devices)),
            pltpu.SemaphoreType.DMA((view_count, tiles)),
            pltpu.SemaphoreType.DMA((view_count, tiles)),
            pltpu.SemaphoreType.DMA((tiles,)),
            pltpu.SemaphoreType.DMA((tiles,)),
        ],
        compiler_params=pltpu.CompilerParams(
            collective_id=1, has_side_effects=True, vmem_limit_bytes=40 * 1024 * 1024
        ),
    )(
        start, fraction, colour_weight * halves[None, :, None], colour_bias * halves, slab_order,
        rimmed, lengths[:, 0, :, None], key_by_channel, key_by_row, warp_matrix,
    )
    return (species_out, frame.reshape(view_count, rows, 4, width))


def solution(mesh):
    in_specs = (
        P(None, "depth", "row", "col"),
        P("depth", "row", "col"),
        P("depth", "row", "col"),
        P(),
        P(),
        P(),
        P(),
        P("depth", "col", "row"),
        P("depth", "col", "row", None),
        P(),
    )
    out_specs = (P(None, "depth", "row", "col"), P("depth", "row", None, "col"))
    return jax.shard_map(body, mesh=mesh, in_specs=in_specs, out_specs=out_specs, check_vma=False)
```

```python
import functools

import jax
import jax.numpy as jnp
from jax import lax
from jax.experimental import pallas as pl
from jax.experimental.pallas import tpu as pltpu
from jax.sharding import PartitionSpec as P

TIME_STEP = 0.1
RAY_STEP = 0.02
VEL_DEPTH = 0.3
VEL_ROW = 0.2
VEL_COL = 0.4


MESH = pl.DeviceIdType.MESH

LAYERS = 3


def advance(
    depth_devices, row_devices, tiles, rim_width,
    species_ref, diffusivity_ref, rate_ref, species_out_ref, shifted,
    deep, first_ref, second_ref, step_ref, row_got, packs, got, stage_out, stage_in, send_sem, recv_sem,
):
    me_d, me_r, me_c = lax.axis_index("depth"), lax.axis_index("row"), lax.axis_index("col")
    depth_cells, rows, width = species_ref.shape[1:]
    tall, wide = rows + 8, 2 * width
    edge = LAYERS + rim_width
    last = LAYERS + depth_cells

    def link(number, src, dst, device):
        return pltpu.make_async_remote_copy(
            src_ref=src, dst_ref=dst, send_sem=send_sem.at[number], recv_sem=recv_sem.at[number],
            device_id=device, device_id_type=MESH,
        )

    def begin(place, count, down, up):
        @pl.when(place > 0)
        def _():
            for copy in down:
                copy.start()

        @pl.when(place < count - 1)
        def _():
            for copy in up:
                copy.start()

    def finish(place, count, down, up, below, above):
        @pl.when(place > 0)
        def _():
            for copy in down:
                copy.wait_send()
            for copy in up:
                copy.wait_recv()

        @pl.when(place < count - 1)
        def _():
            for copy in up:
                copy.wait_send()
            for copy in down:
                copy.wait_recv()

        @pl.when(place == 0)
        def _():
            below[...] = jnp.zeros(below.shape, below.dtype)

        @pl.when(place == count - 1)
        def _():
            above[...] = jnp.zeros(above.shape, above.dtype)

    row_down = (me_d, lax.rem(me_r + row_devices - 1, row_devices), me_c)
    row_up = (me_d, lax.rem(me_r + 1, row_devices), me_c)
    col_down = (me_d, me_r, lax.rem(me_c + tiles - 1, tiles))
    col_up = (me_d, me_r, lax.rem(me_c + 1, tiles))
    depth_down = (lax.rem(me_d + depth_devices - 1, depth_devices), me_r, me_c)
    depth_up = (lax.rem(me_d + 1, depth_devices), me_r, me_c)

    low, high = pl.ds(0, 8), pl.ds(rows - 8, 8)
    down = [
        link(0, species_ref.at[:, :, low], row_got.at[1, pl.ds(0, 2)], row_down),
        link(1, diffusivity_ref.at[:, low], row_got.at[1, 2], row_down),
        link(2, rate_ref.at[:, low], row_got.at[1, 3], row_down),
    ]
    up = [
        link(3, species_ref.at[:, :, high], row_got.at[0, pl.ds(0, 2)], row_up),
        link(4, diffusivity_ref.at[:, high], row_got.at[0, 2], row_up),
        link(5, rate_ref.at[:, high], row_got.at[0, 3], row_up),
    ]
    begin(me_r, row_devices, down, up)

    def place_cells(cell, carry):
        for field in range(2):
            deep[field, LAYERS + cell, pl.ds(0, rows), pl.ds(0, width)] = species_ref[field, cell]
        deep[2, LAYERS + cell, pl.ds(0, rows), pl.ds(0, width)] = diffusivity_ref[cell]
        deep[3, LAYERS + cell, pl.ds(0, rows), pl.ds(0, width)] = rate_ref[cell]
        return carry

    lax.fori_loop(0, depth_cells, place_cells, 0)
    row_at = lax.broadcasted_iota(jnp.int32, (tall, wide), 0)
    row_at = me_r * rows + jnp.where(row_at < rows + 4, row_at, row_at - tall)
    col_at = lax.broadcasted_iota(jnp.int32, (tall, wide), 1)
    col_at = me_c * width + jnp.where(col_at < width + width // 2, col_at, col_at - wide)
    inside = (row_at >= 0) & (row_at < rows * row_devices) & (col_at >= 0) & (col_at < width * tiles)
    step_ref[...] = jnp.where(inside, TIME_STEP, 0.0)
    finish(me_r, row_devices, down, up, row_got.at[0], row_got.at[1])

    near = lax.broadcasted_iota(jnp.int32, (8, width), 0) < 4

    def place_rows(cell, carry):
        for field in range(4):
            deep[field, LAYERS + cell, pl.ds(rows, 8), pl.ds(0, width)] = jnp.where(
                near, row_got[1, field, cell], row_got[0, field, cell]
            )
        return carry

    lax.fori_loop(0, depth_cells, place_rows, 0)

    lane = lax.broadcasted_iota(jnp.int32, (tall, width), 1)

    def turned(array, shift):
        shift = shift % width
        return array if shift == 0 else pltpu.roll(array, shift, 1)

    def pack_columns(field, carry):
        left = jnp.zeros((tall, width), jnp.float32)
        right = left
        for cell in range(depth_cells):
            plane = deep[field, LAYERS + cell, :, pl.ds(0, width)]
            here = (lane >= edge * cell) & (lane < edge * (cell + 1))
            left = jnp.where(here, turned(plane, edge * cell), left)
            right = jnp.where(here, turned(plane, edge * (cell + 1)), right)
        packs[0, field] = left
        packs[1, field] = right
        return carry

    lax.fori_loop(0, 4, pack_columns, 0)
    down = [link(6, packs.at[0], got.at[1], col_down)]
    up = [link(7, packs.at[1], got.at[0], col_up)]
    begin(me_c, tiles, down, up)
    finish(me_c, tiles, down, up, got.at[0], got.at[1])

    def side_tile(below, below_at, above, above_at):
        return jnp.where(
            lane < edge,
            turned(above, -above_at),
            jnp.where(lane >= width - edge, turned(below, width - edge - below_at), 0.0),
        )

    lower = [(f, LAYERS + k, last + k) for f in range(2) for k in range(3)]
    lower += [(f, LAYERS + k, last + k) for f in range(2, 4) for k in range(2)]
    upper = [(f, last - 3 + k, k) for f in range(2) for k in range(3)]
    upper += [(f, last - 3 + k, k) for f in range(2, 4) for k in range(1, 3)]
    span = 3 * edge

    def corner_at(field, side):
        return (field % 2) * (width // 2) + side * (width // 4)

    for way, (items, start) in enumerate(((lower, 0), (upper, edge * (depth_cells - 3)))):
        for pair in range(len(items) // 2):
            planes = [deep[f, here, :, pl.ds(0, width)] for f, here, _ in items[2 * pair : 2 * pair + 2]]
            stage_out[way, pair] = jnp.concatenate(planes, axis=0).astype(jnp.bfloat16)
        corners = []
        for half in range(2):
            tile = jnp.zeros((tall, width), jnp.float32)
            for field in (2 * half, 2 * half + 1):
                for side in range(2):
                    at = corner_at(field, side)
                    here = (lane >= at) & (lane < at + span)
                    tile = jnp.where(here, turned(got[side, field], at - start), tile)
            corners.append(tile)
        stage_out[way, len(items) // 2] = jnp.concatenate(corners, axis=0).astype(jnp.bfloat16)
    down = [link(8, stage_out.at[0], stage_in.at[1], depth_down)]
    up = [link(9, stage_out.at[1], stage_in.at[0], depth_up)]
    begin(me_d, depth_devices, down, up)

    def place_sides(field, carry):
        for cell in range(depth_cells):
            deep[field, LAYERS + cell, :, pl.ds(width, width)] = side_tile(
                got[0, field], edge * cell, got[1, field], edge * cell
            )
        return carry

    lax.fori_loop(0, 4, place_sides, 0)

    def rates_of(source, plane):
        time_step = step_ref[...]
        at = me_d * depth_cells + plane - LAYERS
        time_step = time_step * jnp.where((at >= 0) & (at < depth_cells * depth_devices), 1.0, 0.0)
        fuel, heat = source[0, plane], source[1, plane]
        squared = heat * heat
        burned = deep[3, plane] * fuel * squared / (1.0 + squared)
        spread = deep[2, plane]
        changes = []
        for field, centre in ((0, fuel), (1, heat)):
            below_depth, above_depth = source[field, plane - 1], source[field, plane + 1]
            below_row, above_row = pltpu.roll(centre, 1, 0), pltpu.roll(centre, tall - 1, 0)
            below_col, above_col = pltpu.roll(centre, 1, 1), pltpu.roll(centre, wide - 1, 1)
            laplace = (
                below_depth + above_depth + below_row + above_row + below_col + above_col - 6.0 * centre
            )
            carried = (
                VEL_DEPTH * below_depth + VEL_ROW * below_row + VEL_COL * below_col
                - (VEL_DEPTH + VEL_ROW + VEL_COL) * centre
            )
            total = spread * laplace + carried
            total = total - burned if field == 0 else total + burned
            changes.append(centre + time_step * total)
        return changes

    def first_stage(plane):
        for field, value in enumerate(rates_of(deep, plane)):
            first_ref[field, plane] = value

    def second_stage(plane):
        for field, value in enumerate(rates_of(first_ref, plane)):
            second_ref[field, plane] = 0.75 * deep[field, plane] + 0.25 * value

    def third_stage(plane):
        cell = plane - LAYERS
        for field, value in enumerate(rates_of(second_ref, plane)):
            final = deep[field, plane] * (1.0 / 3.0) + (2.0 / 3.0) * value
            final = final[:rows]
            species_out_ref[field, cell] = final[:, :width]
            earlier = pltpu.roll(final, rim_width, 1)[:, :width]
            for shift in range(2 * rim_width):
                turn = (rim_width - shift - 1) % wide
                later = (final if turn == 0 else pltpu.roll(final, turn, 1))[:, :width]
                shifted[cell, shift, 2 * field] = earlier
                shifted[cell, shift, 2 * field + 1] = later - earlier
                earlier = later

    def inner(stage, begin_at, end_at):
        def one(plane, carry):
            stage(plane)
            return carry

        lax.fori_loop(begin_at, end_at, one, 0)

    def outer(stage, begin_at, gap):
        def one(number, carry):
            stage(begin_at + number + (number // 3) * gap)
            return carry

        lax.fori_loop(0, 6, one, 0)

    inner(first_stage, LAYERS + 1, last - 1)
    inner(second_stage, LAYERS + 2, last - 2)
    inner(third_stage, LAYERS + 3, last - 3)
    finish(me_d, depth_devices, down, up, stage_in.at[0], stage_in.at[1])
    for way, (items, place) in enumerate(((upper, 0), (lower, last))):
        pairs = len(items) // 2
        corners = stage_in[way, pairs].astype(jnp.float32)
        for pair in range(pairs):
            both = stage_in[way, pair].astype(jnp.float32)
            for half in range(2):
                field, _, there = items[2 * pair + half]
                deep[field, there, :, pl.ds(0, width)] = both[half * tall : (half + 1) * tall]
                tile = corners[field // 2 * tall : (field // 2 + 1) * tall]
                layer = edge * (there - place)
                deep[field, there, :, pl.ds(width, width)] = side_tile(
                    tile, corner_at(field, 0) + layer, tile, corner_at(field, 1) + layer
                )
    outer(first_stage, 1, depth_cells - 2)
    outer(second_stage, 2, depth_cells - 4)
    outer(third_stage, 3, depth_cells - 6)


def march_kernel(
    depth_devices, row_devices, tiles, capacity, rim_width,
    start_ref, fraction_ref, weight_ref, bias_ref, order_ref,
    species_ref, diffusivity_ref, rate_ref, length_ref, key_by_channel_ref, key_by_row_ref, warp_ref,
    species_out_ref, frame_ref,
    shifted, *scratch,
):
    view_count = frame_ref.shape[0]
    stacks = scratch[:view_count]
    images = scratch[view_count : 2 * view_count]
    packs = scratch[2 * view_count : 3 * view_count]
    arrivals = scratch[3 * view_count : 4 * view_count]
    keys, slab_send, slab_recv, tile_send, tile_recv, key_send, key_recv = scratch[
        4 * view_count : 4 * view_count + 7
    ]
    advance_scratch = scratch[4 * view_count + 7 :]
    depth_cells, rows, width = shifted.shape[0], shifted.shape[3], shifted.shape[4]
    me_d, me_r, me_c = lax.axis_index("depth"), lax.axis_index("row"), lax.axis_index("col")

    def slab_of(step):
        return lax.rem(me_d + step, depth_devices)

    def tile_of(step):
        return lax.rem(me_c + step, tiles)

    barrier = pltpu.get_barrier_semaphore()
    for step in range(1, depth_devices):
        pl.semaphore_signal(barrier, inc=1, device_id=(slab_of(step), me_r, me_c), device_id_type=MESH)
    for step in range(1, tiles):
        pl.semaphore_signal(barrier, inc=1, device_id=(me_d, me_r, tile_of(step)), device_id_type=MESH)

    row_steps = sorted({1, row_devices - 1})
    for step in row_steps:
        row_peer = lax.rem(me_r + step, row_devices)
        pl.semaphore_signal(barrier, inc=1, device_id=(me_d, row_peer, me_c), device_id_type=MESH)
    pl.semaphore_wait(barrier, depth_devices - 1 + tiles - 1 + len(row_steps))

    key_copies = []
    for step in range(1, tiles):
        copy = pltpu.make_async_remote_copy(
            src_ref=key_by_row_ref, dst_ref=keys.at[me_c],
            send_sem=key_send.at[step], recv_sem=key_recv.at[step],
            device_id=(me_d, me_r, tile_of(step)), device_id_type=MESH,
        )
        copy.start()
        key_copies.append(copy)
    keys[me_c] = key_by_row_ref[...]
    advance(
        depth_devices, row_devices, tiles, rim_width,
        species_ref, diffusivity_ref, rate_ref, species_out_ref, shifted, *advance_scratch,
    )

    def render(view, out_ref):
        weights = [[weight_ref[view, c, f] for f in range(2)] for c in range(4)]
        biases = [bias_ref[view, c] for c in range(4)]

        def cells(cell, state):
            red, green, blue, through = state
            at = start_ref[view, cell]
            fraction = fraction_ref[view, cell]
            s0 = shifted[cell, at, 0] + fraction * shifted[cell, at, 1]
            s1 = shifted[cell, at, 2] + fraction * shifted[cell, at, 3]
            logits = [weights[c][0] * s0 + weights[c][1] * s1 + biases[c] for c in range(4)]
            fading = jnp.exp(-RAY_STEP * jnp.log(1.0 + jnp.exp(logits[3])))
            later = through * fading
            share = through - later
            return (
                red + share * jnp.tanh(logits[0]),
                green + share * jnp.tanh(logits[1]),
                blue + share * jnp.tanh(logits[2]),
                later,
            )

        zero = jnp.zeros((rows, width), jnp.float32)
        red, green, blue, through = lax.fori_loop(
            0, depth_cells, cells, (zero, zero, zero, zero + 1.0), unroll=4
        )
        opacity = 1.0 - through
        out_ref[0] = 0.5 * (red + opacity)
        out_ref[1] = 0.5 * (green + opacity)
        out_ref[2] = 0.5 * (blue + opacity)
        out_ref[3] = opacity

    slots = 4 * capacity

    def render_group(number):
        copies = []
        for step in list(range(1, depth_devices)) + [0]:
            view = slab_of(step) * view_count + number
            if step == 0:
                render(view, stacks[number].at[me_d])
            else:
                render(view, images[number].at[step])
                copy = pltpu.make_async_remote_copy(
                    src_ref=images[number].at[step], dst_ref=stacks[number].at[me_d],
                    send_sem=slab_send.at[number, step], recv_sem=slab_recv.at[number, step],
                    device_id=(slab_of(step), me_r, me_c), device_id_type=MESH,
                )
                copy.start()
                copies.append(copy)
        return copies

    def composite(number):
        view = me_d * view_count + number
        stack = stacks[number]
        result = stack[order_ref[view, 0]]
        for position in range(1, depth_devices):
            result = result + (1.0 - result[3:4]) * stack[order_ref[view, position]]
        keep = lax.broadcasted_iota(jnp.int32, (rows, width), 1) < length_ref[number]
        picture = jnp.where(keep[None], result, 0.0).reshape(4 * rows, width).astype(jnp.bfloat16)
        line = lax.broadcasted_iota(jnp.int32, (tiles * slots, 4 * rows), 0)
        pixel = lax.broadcasted_iota(jnp.int32, (tiles * slots, 4 * rows), 1)
        wanted = (line // slots) * capacity + line % capacity
        key = key_by_channel_ref[number : number + 1, :]
        chosen = (wanted == key) & ((line // capacity) % 4 == pixel // rows)
        packed = jnp.dot(
            jnp.where(chosen, 1.0, 0.0).astype(jnp.bfloat16), picture, preferred_element_type=jnp.float32
        ).astype(jnp.bfloat16)
        packs[number][...] = packed.reshape(tiles, slots, width)
        arrivals[number][me_c] = packs[number][me_c]
        copies = []
        for step in range(1, tiles):
            copy = pltpu.make_async_remote_copy(
                src_ref=packs[number].at[tile_of(step)], dst_ref=arrivals[number].at[me_c],
                send_sem=tile_send.at[number, step], recv_sem=tile_recv.at[number, step],
                device_id=(me_d, me_r, tile_of(step)), device_id_type=MESH,
            )
            copy.start()
            copies.append(copy)
        return copies

    def warp(number):
        line = lax.broadcasted_iota(jnp.int32, (slots, 4 * rows), 0)
        pixel = lax.broadcasted_iota(jnp.int32, (slots, 4 * rows), 1)
        wanted = me_c * capacity + line % capacity
        same = line // capacity == pixel % 4
        places = [
            jnp.where((wanted == keys[tile, number : number + 1, :]) & same, 1.0, 0.0).astype(jnp.bfloat16)
            for tile in range(tiles)
        ]
        gathered = lax.dot_general(
            jnp.concatenate(places, axis=0),
            arrivals[number][...].reshape(tiles * slots, width),
            (((0,), (0,)), ((), ())),
            preferred_element_type=jnp.float32,
        )
        high = gathered.astype(jnp.bfloat16)
        low = (gathered - high.astype(jnp.float32)).astype(jnp.bfloat16)
        matrix = warp_ref[me_d * view_count + number]
        frame_ref[number] = jnp.dot(high, matrix, preferred_element_type=jnp.float32) + jnp.dot(
            low, matrix, preferred_element_type=jnp.float32
        )

    slab_copies, tile_copies = [], []
    for number in range(view_count):
        slab_copies.append(render_group(number))
        if number > 0:
            for copy in slab_copies[number - 1]:
                copy.wait()
            tile_copies.append(composite(number - 1))
    for copy in slab_copies[-1]:
        copy.wait()
    tile_copies.append(composite(view_count - 1))
    for copy in key_copies:
        copy.wait()
    for number in range(view_count):
        for copy in tile_copies[number]:
            copy.wait()
        warp(number)


def slot_keys(owner_rows, capacity):
    rows = owner_rows.shape[-1]
    same = owner_rows[..., :, None] == owner_rows[..., None, :]
    places = jnp.arange(rows, dtype=jnp.int32)
    rank = jnp.sum((same & (places[:, None] < places[None, :])).astype(jnp.int32), axis=-2)
    return owner_rows * capacity + rank


def body(
    species, diffusivity, reaction_rate, shear_rate, colour_weight, colour_bias,
    slab_order, lengths, owners, warp_matrix,
):
    depth_cells, rows, width = species.shape[1:]
    depth_devices = lax.axis_size("depth")
    tiles = lax.axis_size("col")
    depth_total = depth_cells * depth_devices
    rim_width = (4 * depth_total + 99) // 100
    row_devices = lax.axis_size("row")
    planes, tall = depth_cells + 2 * LAYERS, rows + 8
    views = shear_rate.shape[0]
    view_count = views // depth_devices
    capacity = 2 * rows // tiles
    cell_at = lax.axis_index("depth") * depth_cells + jnp.arange(depth_cells, dtype=jnp.int32)
    offset = shear_rate[:, None] * (cell_at.astype(jnp.float32) + 0.5 - 0.5 * depth_total)
    floor_part = jnp.floor(offset)
    fraction = offset - floor_part
    start = jnp.clip(floor_part.astype(jnp.int32) + rim_width, 0, 2 * rim_width - 1)
    halves = jnp.array([0.5, 0.5, 0.5, 1.0], jnp.float32)
    key = slot_keys(owners[:, 0, :, 0], capacity)
    key_by_channel = jnp.tile(key, (1, 4))
    key_by_row = jnp.repeat(key, 4, axis=1)
    slots = 4 * capacity
    vmem = pl.BlockSpec(memory_space=pltpu.VMEM)
    smem = pl.BlockSpec(memory_space=pltpu.SMEM)
    species_out, frame = pl.pallas_call(
        functools.partial(march_kernel, depth_devices, row_devices, tiles, capacity, rim_width),
        out_shape=(
            jax.ShapeDtypeStruct(species.shape, jnp.float32),
            jax.ShapeDtypeStruct((view_count, 4 * rows, width), jnp.float32),
        ),
        in_specs=[smem] * 5 + [vmem] * 7,
        out_specs=(vmem, vmem),
        scratch_shapes=[pltpu.VMEM((depth_cells, 2 * rim_width, 4, rows, width), jnp.float32)]
        + [pltpu.VMEM((depth_devices, 4, rows, width), jnp.float32)] * view_count
        + [pltpu.VMEM((depth_devices, 4, rows, width), jnp.float32)] * view_count
        + [pltpu.VMEM((tiles, slots, width), jnp.bfloat16)] * view_count
        + [pltpu.VMEM((tiles, slots, width), jnp.bfloat16)] * view_count
        + [
            pltpu.VMEM((tiles, view_count, 4 * rows), jnp.int32),
            pltpu.SemaphoreType.DMA((view_count, depth_devices)),
            pltpu.SemaphoreType.DMA((view_count, depth_devices)),
            pltpu.SemaphoreType.DMA((view_count, tiles)),
            pltpu.SemaphoreType.DMA((view_count, tiles)),
            pltpu.SemaphoreType.DMA((tiles,)),
            pltpu.SemaphoreType.DMA((tiles,)),
        ]
        + [
            pltpu.VMEM((4, planes, tall, 2 * width), jnp.float32),
            pltpu.VMEM((2, planes, tall, 2 * width), jnp.float32),
            pltpu.VMEM((2, planes, tall, 2 * width), jnp.float32),
            pltpu.VMEM((tall, 2 * width), jnp.float32),
            pltpu.VMEM((2, 4, depth_cells, 8, width), jnp.float32),
            pltpu.VMEM((2, 4, tall, width), jnp.float32),
            pltpu.VMEM((2, 4, tall, width), jnp.float32),
            pltpu.VMEM((2, 6, 2 * tall, width), jnp.bfloat16),
            pltpu.VMEM((2, 6, 2 * tall, width), jnp.bfloat16),
            pltpu.SemaphoreType.DMA((10,)),
            pltpu.SemaphoreType.DMA((10,)),
        ],
        compiler_params=pltpu.CompilerParams(
            collective_id=1, has_side_effects=True, vmem_limit_bytes=40 * 1024 * 1024
        ),
    )(
        start, fraction, colour_weight * halves[None, :, None], colour_bias * halves, slab_order,
        species, diffusivity, reaction_rate, lengths[:, 0, :, None], key_by_channel, key_by_row, warp_matrix,
    )
    return (species_out, frame.reshape(view_count, rows, 4, width))


def solution(mesh):
    in_specs = (
        P(None, "depth", "row", "col"),
        P("depth", "row", "col"),
        P("depth", "row", "col"),
        P(),
        P(),
        P(),
        P(),
        P("depth", "col", "row"),
        P("depth", "col", "row", None),
        P(),
    )
    out_specs = (P(None, "depth", "row", "col"), P("depth", "row", None, "col"))
    return jax.shard_map(body, mesh=mesh, in_specs=in_specs, out_specs=out_specs, check_vma=False)
```

```python
import functools

import jax
import jax.numpy as jnp
from jax import lax
from jax.experimental import pallas as pl
from jax.experimental.pallas import tpu as pltpu
from jax.sharding import PartitionSpec as P

TIME_STEP = 0.1
RAY_STEP = 0.02
VEL_DEPTH = 0.3
VEL_ROW = 0.2
VEL_COL = 0.4


MESH = pl.DeviceIdType.MESH

LAYERS = 3


def advance(
    depth_devices, row_devices, tiles, rim_width,
    species_ref, diffusivity_ref, rate_ref, species_out_ref, shifted, local_sem,
    deep, first_ref, second_ref, step_ref, row_got, packs, got, stage_out, stage_in, send_sem, recv_sem,
):
    me_d, me_r, me_c = lax.axis_index("depth"), lax.axis_index("row"), lax.axis_index("col")
    depth_cells, rows, width = species_ref.shape[1:]
    tall, wide = rows + 8, 2 * width
    edge = LAYERS + rim_width
    last = LAYERS + depth_cells

    def link(number, src, dst, device):
        return pltpu.make_async_remote_copy(
            src_ref=src, dst_ref=dst, send_sem=send_sem.at[number], recv_sem=recv_sem.at[number],
            device_id=device, device_id_type=MESH,
        )

    def begin(place, count, down, up):
        @pl.when(place > 0)
        def _():
            for copy in down:
                copy.start()

        @pl.when(place < count - 1)
        def _():
            for copy in up:
                copy.start()

    def finish(place, count, down, up, below, above):
        @pl.when(place > 0)
        def _():
            for copy in down:
                copy.wait_send()
            for copy in up:
                copy.wait_recv()

        @pl.when(place < count - 1)
        def _():
            for copy in up:
                copy.wait_send()
            for copy in down:
                copy.wait_recv()

        @pl.when(place == 0)
        def _():
            below[...] = jnp.zeros(below.shape, below.dtype)

        @pl.when(place == count - 1)
        def _():
            above[...] = jnp.zeros(above.shape, above.dtype)

    row_down = (me_d, lax.rem(me_r + row_devices - 1, row_devices), me_c)
    row_up = (me_d, lax.rem(me_r + 1, row_devices), me_c)
    col_down = (me_d, me_r, lax.rem(me_c + tiles - 1, tiles))
    col_up = (me_d, me_r, lax.rem(me_c + 1, tiles))
    depth_down = (lax.rem(me_d + depth_devices - 1, depth_devices), me_r, me_c)
    depth_up = (lax.rem(me_d + 1, depth_devices), me_r, me_c)

    low, high = pl.ds(0, 8), pl.ds(rows - 8, 8)
    down = [
        link(0, species_ref.at[:, :, low], row_got.at[1, pl.ds(0, 2)], row_down),
        link(1, diffusivity_ref.at[:, low], row_got.at[1, 2], row_down),
        link(2, rate_ref.at[:, low], row_got.at[1, 3], row_down),
    ]
    up = [
        link(3, species_ref.at[:, :, high], row_got.at[0, pl.ds(0, 2)], row_up),
        link(4, diffusivity_ref.at[:, high], row_got.at[0, 2], row_up),
        link(5, rate_ref.at[:, high], row_got.at[0, 3], row_up),
    ]
    begin(me_r, row_devices, down, up)

    own = (pl.ds(LAYERS, depth_cells), pl.ds(0, rows), pl.ds(0, width))
    sources = (species_ref.at[0], species_ref.at[1], diffusivity_ref, rate_ref)
    local = [
        pltpu.make_async_copy(source, deep.at[(field, *own)], local_sem.at[2 + field])
        for field, source in enumerate(sources)
    ]
    for copy in local:
        copy.start()
    row_at = lax.broadcasted_iota(jnp.int32, (tall, wide), 0)
    row_at = me_r * rows + jnp.where(row_at < rows + 4, row_at, row_at - tall)
    col_at = lax.broadcasted_iota(jnp.int32, (tall, wide), 1)
    col_at = me_c * width + jnp.where(col_at < width + width // 2, col_at, col_at - wide)
    inside = (row_at >= 0) & (row_at < rows * row_devices) & (col_at >= 0) & (col_at < width * tiles)
    step_ref[...] = jnp.where(inside, TIME_STEP, 0.0)
    finish(me_r, row_devices, down, up, row_got.at[0], row_got.at[1])

    for copy in local:
        copy.wait()
    near = lax.broadcasted_iota(jnp.int32, (8, width), 0) < 4

    def place_rows(cell, carry):
        for field in range(4):
            deep[field, LAYERS + cell, pl.ds(rows, 8), pl.ds(0, width)] = jnp.where(
                near, row_got[1, field, cell], row_got[0, field, cell]
            )
        return carry

    lax.fori_loop(0, depth_cells, place_rows, 0)

    lane = lax.broadcasted_iota(jnp.int32, (tall, width), 1)

    def turned(array, shift):
        shift = shift % width
        return array if shift == 0 else pltpu.roll(array, shift, 1)

    def pack_columns(field, carry):
        left = jnp.zeros((tall, width), jnp.float32)
        right = left
        for cell in range(depth_cells):
            plane = deep[field, LAYERS + cell, :, pl.ds(0, width)]
            here = (lane >= edge * cell) & (lane < edge * (cell + 1))
            left = jnp.where(here, turned(plane, edge * cell), left)
            right = jnp.where(here, turned(plane, edge * (cell + 1)), right)
        packs[0, field] = left
        packs[1, field] = right
        return carry

    lax.fori_loop(0, 4, pack_columns, 0)
    down = [link(6, packs.at[0], got.at[1], col_down)]
    up = [link(7, packs.at[1], got.at[0], col_up)]
    begin(me_c, tiles, down, up)
    finish(me_c, tiles, down, up, got.at[0], got.at[1])

    def side_tile(below, below_at, above, above_at):
        return jnp.where(
            lane < edge,
            turned(above, -above_at),
            jnp.where(lane >= width - edge, turned(below, width - edge - below_at), 0.0),
        )

    lower = [(f, LAYERS + k, last + k) for f in range(2) for k in range(3)]
    lower += [(f, LAYERS + k, last + k) for f in range(2, 4) for k in range(2)]
    upper = [(f, last - 3 + k, k) for f in range(2) for k in range(3)]
    upper += [(f, last - 3 + k, k) for f in range(2, 4) for k in range(1, 3)]
    span = 3 * edge

    def corner_at(field, side):
        return (field % 2) * (width // 2) + side * (width // 4)

    for way, (items, start) in enumerate(((lower, 0), (upper, edge * (depth_cells - 3)))):
        for pair in range(len(items) // 2):
            planes = [deep[f, here, :, pl.ds(0, width)] for f, here, _ in items[2 * pair : 2 * pair + 2]]
            stage_out[way, pair] = jnp.concatenate(planes, axis=0).astype(jnp.bfloat16)
        corners = []
        for half in range(2):
            tile = jnp.zeros((tall, width), jnp.float32)
            for field in (2 * half, 2 * half + 1):
                for side in range(2):
                    at = corner_at(field, side)
                    here = (lane >= at) & (lane < at + span)
                    tile = jnp.where(here, turned(got[side, field], at - start), tile)
            corners.append(tile)
        stage_out[way, len(items) // 2] = jnp.concatenate(corners, axis=0).astype(jnp.bfloat16)
    down = [link(8, stage_out.at[0], stage_in.at[1], depth_down)]
    up = [link(9, stage_out.at[1], stage_in.at[0], depth_up)]
    begin(me_d, depth_devices, down, up)

    def place_sides(field, carry):
        for cell in range(depth_cells):
            deep[field, LAYERS + cell, :, pl.ds(width, width)] = side_tile(
                got[0, field], edge * cell, got[1, field], edge * cell
            )
        return carry

    lax.fori_loop(0, 4, place_sides, 0)

    def rates_of(source, plane):
        time_step = step_ref[...]
        at = me_d * depth_cells + plane - LAYERS
        time_step = time_step * jnp.where((at >= 0) & (at < depth_cells * depth_devices), 1.0, 0.0)
        fuel, heat = source[0, plane], source[1, plane]
        squared = heat * heat
        burned = deep[3, plane] * fuel * squared / (1.0 + squared)
        spread = deep[2, plane]
        changes = []
        for field, centre in ((0, fuel), (1, heat)):
            below_depth, above_depth = source[field, plane - 1], source[field, plane + 1]
            below_row, above_row = pltpu.roll(centre, 1, 0), pltpu.roll(centre, tall - 1, 0)
            below_col, above_col = pltpu.roll(centre, 1, 1), pltpu.roll(centre, wide - 1, 1)
            laplace = (
                below_depth + above_depth + below_row + above_row + below_col + above_col - 6.0 * centre
            )
            carried = (
                VEL_DEPTH * below_depth + VEL_ROW * below_row + VEL_COL * below_col
                - (VEL_DEPTH + VEL_ROW + VEL_COL) * centre
            )
            total = spread * laplace + carried
            total = total - burned if field == 0 else total + burned
            changes.append(centre + time_step * total)
        return changes

    def first_stage(plane):
        for field, value in enumerate(rates_of(deep, plane)):
            first_ref[field, plane] = value

    def second_stage(plane):
        for field, value in enumerate(rates_of(first_ref, plane)):
            second_ref[field, plane] = 0.75 * deep[field, plane] + 0.25 * value

    def third_stage(plane):
        cell = plane - LAYERS
        for field, value in enumerate(rates_of(second_ref, plane)):
            final = deep[field, plane] * (1.0 / 3.0) + (2.0 / 3.0) * value
            final = final[:rows]
            species_out_ref[field, cell] = final[:, :width]
            earlier = pltpu.roll(final, rim_width, 1)[:, :width]
            for shift in range(2 * rim_width):
                turn = (rim_width - shift - 1) % wide
                later = (final if turn == 0 else pltpu.roll(final, turn, 1))[:, :width]
                shifted[cell, shift, 2 * field] = earlier
                shifted[cell, shift, 2 * field + 1] = later - earlier
                earlier = later

    def inner(stage, begin_at, end_at):
        def one(plane, carry):
            stage(plane)
            return carry

        lax.fori_loop(begin_at, end_at, one, 0)

    def outer(stage, begin_at, gap):
        def one(number, carry):
            stage(begin_at + number + (number // 3) * gap)
            return carry

        lax.fori_loop(0, 6, one, 0)

    inner(first_stage, LAYERS + 1, last - 1)
    inner(second_stage, LAYERS + 2, last - 2)
    inner(third_stage, LAYERS + 3, last - 3)
    finish(me_d, depth_devices, down, up, stage_in.at[0], stage_in.at[1])
    for way, (items, place) in enumerate(((upper, 0), (lower, last))):
        pairs = len(items) // 2
        corners = stage_in[way, pairs].astype(jnp.float32)
        for pair in range(pairs):
            both = stage_in[way, pair].astype(jnp.float32)
            for half in range(2):
                field, _, there = items[2 * pair + half]
                deep[field, there, :, pl.ds(0, width)] = both[half * tall : (half + 1) * tall]
                tile = corners[field // 2 * tall : (field // 2 + 1) * tall]
                layer = edge * (there - place)
                deep[field, there, :, pl.ds(width, width)] = side_tile(
                    tile, corner_at(field, 0) + layer, tile, corner_at(field, 1) + layer
                )
    outer(first_stage, 1, depth_cells - 2)
    outer(second_stage, 2, depth_cells - 4)
    outer(third_stage, 3, depth_cells - 6)


def march_kernel(
    depth_devices, row_devices, tiles, capacity, rim_width,
    real_ref, whole_ref,
    species_ref, diffusivity_ref, rate_ref, line_ref, warp_hbm,
    species_hbm, frame_hbm,
    shifted, *scratch,
):
    view_count = frame_hbm.shape[0]
    stacks = scratch[:view_count]
    images = scratch[view_count : 2 * view_count]
    packs = scratch[2 * view_count : 3 * view_count]
    arrivals = scratch[3 * view_count : 4 * view_count]
    (
        keys, key_by_channel_ref, key_by_row_ref, warp_ref, species_out_ref, frame_ref,
        slab_send, slab_recv, tile_send, tile_recv, key_send, key_recv, local_sem,
    ) = scratch[4 * view_count : 4 * view_count + 13]
    advance_scratch = scratch[4 * view_count + 13 :]
    depth_cells, rows, width = shifted.shape[0], shifted.shape[3], shifted.shape[4]
    me_d, me_r, me_c = lax.axis_index("depth"), lax.axis_index("row"), lax.axis_index("col")

    def slab_of(step):
        return lax.rem(me_d + step, depth_devices)

    def tile_of(step):
        return lax.rem(me_c + step, tiles)

    barrier = pltpu.get_barrier_semaphore()
    for step in range(1, depth_devices):
        pl.semaphore_signal(barrier, inc=1, device_id=(slab_of(step), me_r, me_c), device_id_type=MESH)
    for step in range(1, tiles):
        pl.semaphore_signal(barrier, inc=1, device_id=(me_d, me_r, tile_of(step)), device_id_type=MESH)

    row_steps = sorted({1, row_devices - 1})
    for step in row_steps:
        row_peer = lax.rem(me_r + step, row_devices)
        pl.semaphore_signal(barrier, inc=1, device_id=(me_d, row_peer, me_c), device_id_type=MESH)
    warp_copy = pltpu.make_async_copy(
        warp_hbm.at[pl.ds(me_d * view_count, view_count)], warp_ref, local_sem.at[0]
    )
    warp_copy.start()
    pixels = 4 * rows
    earlier = lax.broadcasted_iota(jnp.int32, (pixels, pixels), 0)
    later = lax.broadcasted_iota(jnp.int32, (pixels, pixels), 1)
    for target, base, same in (
        (key_by_channel_ref, 0, earlier // rows == later // rows),
        (key_by_row_ref, view_count, earlier % 4 == later % 4),
    ):
        for number in range(view_count):
            owner = line_ref[base + number : base + number + 1, :]
            column = jnp.sum(jnp.where(earlier == later, owner, 0), axis=1, keepdims=True)
            before = (column == owner) & same & (earlier < later)
            rank = jnp.sum(jnp.where(before, 1, 0), axis=0, keepdims=True)
            target[number : number + 1, :] = owner * capacity + rank
    pl.semaphore_wait(barrier, depth_devices - 1 + tiles - 1 + len(row_steps))

    key_copies = []
    for step in range(1, tiles):
        copy = pltpu.make_async_remote_copy(
            src_ref=key_by_row_ref, dst_ref=keys.at[me_c],
            send_sem=key_send.at[step], recv_sem=key_recv.at[step],
            device_id=(me_d, me_r, tile_of(step)), device_id_type=MESH,
        )
        copy.start()
        key_copies.append(copy)
    keys[me_c] = key_by_row_ref[...]
    advance(
        depth_devices, row_devices, tiles, rim_width,
        species_ref, diffusivity_ref, rate_ref, species_out_ref, shifted, local_sem, *advance_scratch,
    )
    species_copy = pltpu.make_async_copy(species_out_ref, species_hbm, local_sem.at[1])
    species_copy.start()

    def render(view, out_ref):
        weights = [[real_ref[view, 2 * c + f] for f in range(2)] for c in range(4)]
        biases = [real_ref[view, 8 + c] for c in range(4)]

        def cells(cell, state):
            red, green, blue, through = state
            at = whole_ref[view, cell]
            fraction = real_ref[view, 12 + cell]
            s0 = shifted[cell, at, 0] + fraction * shifted[cell, at, 1]
            s1 = shifted[cell, at, 2] + fraction * shifted[cell, at, 3]
            logits = [weights[c][0] * s0 + weights[c][1] * s1 + biases[c] for c in range(4)]
            fading = jnp.exp(-RAY_STEP * jnp.log(1.0 + jnp.exp(logits[3])))
            later = through * fading
            share = through - later
            return (
                red + share * jnp.tanh(logits[0]),
                green + share * jnp.tanh(logits[1]),
                blue + share * jnp.tanh(logits[2]),
                later,
            )

        zero = jnp.zeros((rows, width), jnp.float32)
        red, green, blue, through = lax.fori_loop(
            0, depth_cells, cells, (zero, zero, zero, zero + 1.0), unroll=4
        )
        opacity = 1.0 - through
        for channel, value in enumerate((red, green, blue, opacity)):
            value = value if channel == 3 else 0.5 * (value + opacity)
            root = jnp.sqrt(jnp.sqrt(jnp.clip(value, 0.0, 1.0)))
            out_ref[channel] = ((root * 65535.0 + 0.5).astype(jnp.int32) - 32768).astype(jnp.int16)

    slots = 4 * capacity

    def render_group(number):
        copies = []
        for step in list(range(1, depth_devices)) + [0]:
            view = slab_of(step) * view_count + number
            if step == 0:
                render(view, stacks[number].at[me_d])
            else:
                render(view, images[number].at[step])
                copy = pltpu.make_async_remote_copy(
                    src_ref=images[number].at[step], dst_ref=stacks[number].at[me_d],
                    send_sem=slab_send.at[number, step], recv_sem=slab_recv.at[number, step],
                    device_id=(slab_of(step), me_r, me_c), device_id_type=MESH,
                )
                copy.start()
                copies.append(copy)
        return copies

    def composite(number):
        view = me_d * view_count + number
        stack = stacks[number]

        def slab_at(position):
            code = stack[whole_ref[view, depth_cells + position]].astype(jnp.int32)
            root = (code + 32768).astype(jnp.float32) * (1.0 / 65535.0)
            root = root * root
            return root * root

        result = slab_at(0)
        for position in range(1, depth_devices):
            result = result + (1.0 - result[3:4]) * slab_at(position)
        lane = lax.broadcasted_iota(jnp.int32, (rows, width), 1)
        at = lax.broadcasted_iota(jnp.int32, (rows, 4 * rows), 1)
        at = at == lax.broadcasted_iota(jnp.int32, (rows, 4 * rows), 0)
        length = line_ref[2 * view_count + number : 2 * view_count + number + 1, :]
        keep = lane < jnp.sum(jnp.where(at, length, 0), axis=1, keepdims=True)
        picture = jnp.where(keep[None], result, 0.0).reshape(4 * rows, width).astype(jnp.bfloat16)
        line = lax.broadcasted_iota(jnp.int32, (tiles * slots, 4 * rows), 0)
        pixel = lax.broadcasted_iota(jnp.int32, (tiles * slots, 4 * rows), 1)
        wanted = (line // slots) * capacity + line % capacity
        key = key_by_channel_ref[number : number + 1, :]
        chosen = (wanted == key) & ((line // capacity) % 4 == pixel // rows)
        packed = jnp.dot(
            jnp.where(chosen, 1.0, 0.0).astype(jnp.bfloat16), picture, preferred_element_type=jnp.float32
        ).astype(jnp.bfloat16)
        packs[number][...] = packed.reshape(tiles, slots, width)
        arrivals[number][me_c] = packs[number][me_c]
        copies = []
        for step in range(1, tiles):
            copy = pltpu.make_async_remote_copy(
                src_ref=packs[number].at[tile_of(step)], dst_ref=arrivals[number].at[me_c],
                send_sem=tile_send.at[number, step], recv_sem=tile_recv.at[number, step],
                device_id=(me_d, me_r, tile_of(step)), device_id_type=MESH,
            )
            copy.start()
            copies.append(copy)
        return copies

    def warp(number):
        line = lax.broadcasted_iota(jnp.int32, (slots, 4 * rows), 0)
        pixel = lax.broadcasted_iota(jnp.int32, (slots, 4 * rows), 1)
        wanted = me_c * capacity + line % capacity
        same = line // capacity == pixel % 4
        places = [
            jnp.where((wanted == keys[tile, number : number + 1, :]) & same, 1.0, 0.0).astype(jnp.bfloat16)
            for tile in range(tiles)
        ]
        gathered = lax.dot_general(
            jnp.concatenate(places, axis=0),
            arrivals[number][...].reshape(tiles * slots, width),
            (((0,), (0,)), ((), ())),
            preferred_element_type=jnp.float32,
        )
        high = gathered.astype(jnp.bfloat16)
        low = (gathered - high.astype(jnp.float32)).astype(jnp.bfloat16)
        matrix = warp_ref[number]
        frame_ref[number] = jnp.dot(high, matrix, preferred_element_type=jnp.float32) + jnp.dot(
            low, matrix, preferred_element_type=jnp.float32
        )

    slab_copies, tile_copies, frame_copies = [], [], []
    for number in range(view_count):
        slab_copies.append(render_group(number))
        if number > 0:
            for copy in slab_copies[number - 1]:
                copy.wait()
            tile_copies.append(composite(number - 1))
    for copy in slab_copies[-1]:
        copy.wait()
    tile_copies.append(composite(view_count - 1))
    for copy in key_copies:
        copy.wait()
    for number in range(view_count):
        for copy in tile_copies[number]:
            copy.wait()
        if number == 0:
            warp_copy.wait()
        warp(number)
        copy = pltpu.make_async_copy(frame_ref.at[number], frame_hbm.at[number], local_sem.at[6 + number])
        copy.start()
        frame_copies.append(copy)
    for copy in [species_copy] + frame_copies:
        copy.wait()


def body(
    species, diffusivity, reaction_rate, shear_rate, colour_weight, colour_bias,
    slab_order, lengths, owners, warp_matrix,
):
    depth_cells, rows, width = species.shape[1:]
    depth_devices = lax.axis_size("depth")
    tiles = lax.axis_size("col")
    depth_total = depth_cells * depth_devices
    rim_width = (4 * depth_total + 99) // 100
    row_devices = lax.axis_size("row")
    planes, tall = depth_cells + 2 * LAYERS, rows + 8
    views = shear_rate.shape[0]
    view_count = views // depth_devices
    capacity = 2 * rows // tiles
    cell_at = lax.axis_index("depth") * depth_cells + jnp.arange(depth_cells, dtype=jnp.int32)
    offset = shear_rate[:, None] * (cell_at.astype(jnp.float32) + 0.5 - 0.5 * depth_total)
    floor_part = jnp.floor(offset)
    fraction = offset - floor_part
    start = jnp.clip(floor_part.astype(jnp.int32) + rim_width, 0, 2 * rim_width - 1)
    halves = jnp.array([0.5, 0.5, 0.5, 1.0], jnp.float32)
    real = jnp.concatenate(
        [(colour_weight * halves[None, :, None]).reshape(views, 8), colour_bias * halves, fraction], axis=1
    )
    whole = jnp.concatenate([start, slab_order], axis=1)
    owner = owners[:, 0, :, 0]
    lines = jnp.concatenate(
        [jnp.tile(owner, (1, 4)), jnp.repeat(owner, 4, axis=1), jnp.tile(lengths[:, 0, :], (1, 4))], axis=0
    )
    slots = 4 * capacity
    vmem = pl.BlockSpec(memory_space=pltpu.VMEM)
    hbm = pl.BlockSpec(memory_space=pltpu.HBM)
    smem = pl.BlockSpec(memory_space=pltpu.SMEM)
    species_out, frame = pl.pallas_call(
        functools.partial(march_kernel, depth_devices, row_devices, tiles, capacity, rim_width),
        out_shape=(
            jax.ShapeDtypeStruct(species.shape, jnp.float32),
            jax.ShapeDtypeStruct((view_count, 4 * rows, width), jnp.float32),
        ),
        in_specs=[smem] * 2 + [hbm] * 3 + [vmem, hbm],
        out_specs=(hbm, hbm),
        scratch_shapes=[pltpu.VMEM((depth_cells, 2 * rim_width, 4, rows, width), jnp.float32)]
        + [pltpu.VMEM((depth_devices, 4, rows, width), jnp.int16)] * view_count
        + [pltpu.VMEM((depth_devices, 4, rows, width), jnp.int16)] * view_count
        + [pltpu.VMEM((tiles, slots, width), jnp.bfloat16)] * view_count
        + [pltpu.VMEM((tiles, slots, width), jnp.bfloat16)] * view_count
        + [
            pltpu.VMEM((tiles, view_count, 4 * rows), jnp.int32),
            pltpu.VMEM((view_count, 4 * rows), jnp.int32),
            pltpu.VMEM((view_count, 4 * rows), jnp.int32),
            pltpu.VMEM((view_count, *warp_matrix.shape[1:]), warp_matrix.dtype),
            pltpu.VMEM(species.shape, jnp.float32),
            pltpu.VMEM((view_count, 4 * rows, width), jnp.float32),
            pltpu.SemaphoreType.DMA((view_count, depth_devices)),
            pltpu.SemaphoreType.DMA((view_count, depth_devices)),
            pltpu.SemaphoreType.DMA((view_count, tiles)),
            pltpu.SemaphoreType.DMA((view_count, tiles)),
            pltpu.SemaphoreType.DMA((tiles,)),
            pltpu.SemaphoreType.DMA((tiles,)),
            pltpu.SemaphoreType.DMA((6 + view_count,)),
        ]
        + [
            pltpu.VMEM((4, planes, tall, 2 * width), jnp.float32),
            pltpu.VMEM((2, planes, tall, 2 * width), jnp.float32),
            pltpu.VMEM((2, planes, tall, 2 * width), jnp.float32),
            pltpu.VMEM((tall, 2 * width), jnp.float32),
            pltpu.VMEM((2, 4, depth_cells, 8, width), jnp.float32),
            pltpu.VMEM((2, 4, tall, width), jnp.float32),
            pltpu.VMEM((2, 4, tall, width), jnp.float32),
            pltpu.VMEM((2, 6, 2 * tall, width), jnp.bfloat16),
            pltpu.VMEM((2, 6, 2 * tall, width), jnp.bfloat16),
            pltpu.SemaphoreType.DMA((10,)),
            pltpu.SemaphoreType.DMA((10,)),
        ],
        compiler_params=pltpu.CompilerParams(
            collective_id=1, has_side_effects=True, vmem_limit_bytes=40 * 1024 * 1024
        ),
    )(
        real, whole, species, diffusivity, reaction_rate, lines, warp_matrix,
    )
    return (species_out, frame.reshape(view_count, rows, 4, width))


def solution(mesh):
    in_specs = (
        P(None, "depth", "row", "col"),
        P("depth", "row", "col"),
        P("depth", "row", "col"),
        P(),
        P(),
        P(),
        P(),
        P("depth", "col", "row"),
        P("depth", "col", "row", None),
        P(),
    )
    out_specs = (P(None, "depth", "row", "col"), P("depth", "row", None, "col"))
    return jax.shard_map(body, mesh=mesh, in_specs=in_specs, out_specs=out_specs, check_vma=False)
```

```python
import functools

import jax
import jax.numpy as jnp
from jax import lax
from jax.experimental import pallas as pl
from jax.experimental.pallas import tpu as pltpu
from jax.sharding import PartitionSpec as P

TIME_STEP = 0.1
RAY_STEP = 0.02
VEL_DEPTH = 0.3
VEL_ROW = 0.2
VEL_COL = 0.4


MESH = pl.DeviceIdType.MESH

LAYERS = 3


def advance(
    depth_devices, row_devices, tiles, rim_width,
    species_ref, diffusivity_ref, rate_ref, species_out_ref, shifted, local_sem,
    deep, first_ref, second_ref, step_ref, row_got, packs, got, stage_out, stage_in, send_sem, recv_sem,
):
    me_d, me_r, me_c = lax.axis_index("depth"), lax.axis_index("row"), lax.axis_index("col")
    depth_cells, rows, width = species_ref.shape[1:]
    tall, wide = rows + 8, 2 * width
    edge = LAYERS + rim_width
    last = LAYERS + depth_cells

    def link(number, src, dst, device):
        return pltpu.make_async_remote_copy(
            src_ref=src, dst_ref=dst, send_sem=send_sem.at[number], recv_sem=recv_sem.at[number],
            device_id=device, device_id_type=MESH,
        )

    def begin(place, count, down, up):
        @pl.when(place > 0)
        def _():
            for copy in down:
                copy.start()

        @pl.when(place < count - 1)
        def _():
            for copy in up:
                copy.start()

    def finish(place, count, down, up, below, above):
        @pl.when(place > 0)
        def _():
            for copy in down:
                copy.wait_send()
            for copy in up:
                copy.wait_recv()

        @pl.when(place < count - 1)
        def _():
            for copy in up:
                copy.wait_send()
            for copy in down:
                copy.wait_recv()

        @pl.when(place == 0)
        def _():
            below[...] = jnp.zeros(below.shape, below.dtype)

        @pl.when(place == count - 1)
        def _():
            above[...] = jnp.zeros(above.shape, above.dtype)

    row_down = (me_d, lax.rem(me_r + row_devices - 1, row_devices), me_c)
    row_up = (me_d, lax.rem(me_r + 1, row_devices), me_c)
    col_down = (me_d, me_r, lax.rem(me_c + tiles - 1, tiles))
    col_up = (me_d, me_r, lax.rem(me_c + 1, tiles))
    depth_down = (lax.rem(me_d + depth_devices - 1, depth_devices), me_r, me_c)
    depth_up = (lax.rem(me_d + 1, depth_devices), me_r, me_c)

    low, high = pl.ds(0, 8), pl.ds(rows - 8, 8)
    down = [
        link(0, species_ref.at[:, :, low], row_got.at[1, pl.ds(0, 2)], row_down),
        link(1, diffusivity_ref.at[:, low], row_got.at[1, 2], row_down),
        link(2, rate_ref.at[:, low], row_got.at[1, 3], row_down),
    ]
    up = [
        link(3, species_ref.at[:, :, high], row_got.at[0, pl.ds(0, 2)], row_up),
        link(4, diffusivity_ref.at[:, high], row_got.at[0, 2], row_up),
        link(5, rate_ref.at[:, high], row_got.at[0, 3], row_up),
    ]
    begin(me_r, row_devices, down, up)

    own = (pl.ds(LAYERS, depth_cells), pl.ds(0, rows), pl.ds(0, width))
    sources = (species_ref.at[0], species_ref.at[1], diffusivity_ref, rate_ref)
    local = [
        pltpu.make_async_copy(source, deep.at[(field, *own)], local_sem.at[2 + field])
        for field, source in enumerate(sources)
    ]
    for copy in local:
        copy.start()
    row_at = lax.broadcasted_iota(jnp.int32, (tall, wide), 0)
    row_at = me_r * rows + jnp.where(row_at < rows + 4, row_at, row_at - tall)
    col_at = lax.broadcasted_iota(jnp.int32, (tall, wide), 1)
    col_at = me_c * width + jnp.where(col_at < width + width // 2, col_at, col_at - wide)
    inside = (row_at >= 0) & (row_at < rows * row_devices) & (col_at >= 0) & (col_at < width * tiles)
    step_ref[...] = jnp.where(inside, TIME_STEP, 0.0)
    finish(me_r, row_devices, down, up, row_got.at[0], row_got.at[1])

    for copy in local:
        copy.wait()
    near = lax.broadcasted_iota(jnp.int32, (8, width), 0) < 4

    def place_rows(cell, carry):
        for field in range(4):
            deep[field, LAYERS + cell, pl.ds(rows, 8), pl.ds(0, width)] = jnp.where(
                near, row_got[1, field, cell], row_got[0, field, cell]
            )
        return carry

    lax.fori_loop(0, depth_cells, place_rows, 0)

    lane = lax.broadcasted_iota(jnp.int32, (tall, width), 1)

    def turned(array, shift):
        shift = shift % width
        return array if shift == 0 else pltpu.roll(array, shift, 1)

    def pack_columns(field, carry):
        left = jnp.zeros((tall, width), jnp.float32)
        right = left
        for cell in range(depth_cells):
            plane = deep[field, LAYERS + cell, :, pl.ds(0, width)]
            here = (lane >= edge * cell) & (lane < edge * (cell + 1))
            left = jnp.where(here, turned(plane, edge * cell), left)
            right = jnp.where(here, turned(plane, edge * (cell + 1)), right)
        packs[0, field] = left
        packs[1, field] = right
        return carry

    lax.fori_loop(0, 4, pack_columns, 0)
    down = [link(6, packs.at[0], got.at[1], col_down)]
    up = [link(7, packs.at[1], got.at[0], col_up)]
    begin(me_c, tiles, down, up)
    finish(me_c, tiles, down, up, got.at[0], got.at[1])

    def side_tile(below, below_at, above, above_at):
        return jnp.where(
            lane < edge,
            turned(above, -above_at),
            jnp.where(lane >= width - edge, turned(below, width - edge - below_at), 0.0),
        )

    lower = [(f, LAYERS + k, last + k) for f in range(2) for k in range(3)]
    lower += [(f, LAYERS + k, last + k) for f in range(2, 4) for k in range(2)]
    upper = [(f, last - 3 + k, k) for f in range(2) for k in range(3)]
    upper += [(f, last - 3 + k, k) for f in range(2, 4) for k in range(1, 3)]
    span = 3 * edge

    def corner_at(field, side):
        return (field % 2) * (width // 2) + side * (width // 4)

    for way, (items, start) in enumerate(((lower, 0), (upper, edge * (depth_cells - 3)))):
        for pair in range(len(items) // 2):
            planes = [deep[f, here, :, pl.ds(0, width)] for f, here, _ in items[2 * pair : 2 * pair + 2]]
            stage_out[way, pair] = jnp.concatenate(planes, axis=0).astype(jnp.bfloat16)
        corners = []
        for half in range(2):
            tile = jnp.zeros((tall, width), jnp.float32)
            for field in (2 * half, 2 * half + 1):
                for side in range(2):
                    at = corner_at(field, side)
                    here = (lane >= at) & (lane < at + span)
                    tile = jnp.where(here, turned(got[side, field], at - start), tile)
            corners.append(tile)
        stage_out[way, len(items) // 2] = jnp.concatenate(corners, axis=0).astype(jnp.bfloat16)
    down = [link(8, stage_out.at[0], stage_in.at[1], depth_down)]
    up = [link(9, stage_out.at[1], stage_in.at[0], depth_up)]
    begin(me_d, depth_devices, down, up)

    def place_sides(field, carry):
        for cell in range(depth_cells):
            deep[field, LAYERS + cell, :, pl.ds(width, width)] = side_tile(
                got[0, field], edge * cell, got[1, field], edge * cell
            )
        return carry

    lax.fori_loop(0, 4, place_sides, 0)

    def rates_of(source, plane):
        time_step = step_ref[...]
        at = me_d * depth_cells + plane - LAYERS
        time_step = time_step * jnp.where((at >= 0) & (at < depth_cells * depth_devices), 1.0, 0.0)
        fuel, heat = source[0, plane], source[1, plane]
        squared = heat * heat
        burned = deep[3, plane] * fuel * squared / (1.0 + squared)
        spread = deep[2, plane]
        changes = []
        for field, centre in ((0, fuel), (1, heat)):
            below_depth, above_depth = source[field, plane - 1], source[field, plane + 1]
            below_row, above_row = pltpu.roll(centre, 1, 0), pltpu.roll(centre, tall - 1, 0)
            below_col, above_col = pltpu.roll(centre, 1, 1), pltpu.roll(centre, wide - 1, 1)
            laplace = (
                below_depth + above_depth + below_row + above_row + below_col + above_col - 6.0 * centre
            )
            carried = (
                VEL_DEPTH * below_depth + VEL_ROW * below_row + VEL_COL * below_col
                - (VEL_DEPTH + VEL_ROW + VEL_COL) * centre
            )
            total = spread * laplace + carried
            total = total - burned if field == 0 else total + burned
            changes.append(centre + time_step * total)
        return changes

    def first_stage(plane):
        for field, value in enumerate(rates_of(deep, plane)):
            first_ref[field, plane] = value

    def second_stage(plane):
        for field, value in enumerate(rates_of(first_ref, plane)):
            second_ref[field, plane] = 0.75 * deep[field, plane] + 0.25 * value

    def third_stage(plane):
        cell = plane - LAYERS
        for field, value in enumerate(rates_of(second_ref, plane)):
            final = deep[field, plane] * (1.0 / 3.0) + (2.0 / 3.0) * value
            final = final[:rows]
            species_out_ref[field, cell] = final[:, :width]
            earlier = pltpu.roll(final, rim_width, 1)[:, :width]
            for shift in range(2 * rim_width):
                turn = (rim_width - shift - 1) % wide
                later = (final if turn == 0 else pltpu.roll(final, turn, 1))[:, :width]
                shifted[cell, shift, 2 * field] = earlier
                shifted[cell, shift, 2 * field + 1] = later - earlier
                earlier = later

    def inner(stage, begin_at, end_at):
        def one(plane, carry):
            stage(plane)
            return carry

        lax.fori_loop(begin_at, end_at, one, 0)

    def outer(stage, begin_at, gap):
        def one(number, carry):
            stage(begin_at + number + (number // 3) * gap)
            return carry

        lax.fori_loop(0, 6, one, 0)

    inner(first_stage, LAYERS + 1, last - 1)
    inner(second_stage, LAYERS + 2, last - 2)
    inner(third_stage, LAYERS + 3, last - 3)
    finish(me_d, depth_devices, down, up, stage_in.at[0], stage_in.at[1])
    for way, (items, place) in enumerate(((upper, 0), (lower, last))):
        pairs = len(items) // 2
        corners = stage_in[way, pairs].astype(jnp.float32)
        for pair in range(pairs):
            both = stage_in[way, pair].astype(jnp.float32)
            for half in range(2):
                field, _, there = items[2 * pair + half]
                deep[field, there, :, pl.ds(0, width)] = both[half * tall : (half + 1) * tall]
                tile = corners[field // 2 * tall : (field // 2 + 1) * tall]
                layer = edge * (there - place)
                deep[field, there, :, pl.ds(width, width)] = side_tile(
                    tile, corner_at(field, 0) + layer, tile, corner_at(field, 1) + layer
                )
    outer(first_stage, 1, depth_cells - 2)
    outer(second_stage, 2, depth_cells - 4)
    outer(third_stage, 3, depth_cells - 6)


def march_kernel(
    depth_devices, row_devices, tiles, capacity, rim_width,
    shear_ref, weight_ref, bias_ref, start_ref, order_ref,
    species_ref, diffusivity_ref, rate_ref, owner_ref, length_ref, warp_hbm,
    species_hbm, frame_hbm,
    shifted, *scratch,
):
    view_count = frame_hbm.shape[0]
    stacks = scratch[:view_count]
    images = scratch[view_count : 2 * view_count]
    packs = scratch[2 * view_count : 3 * view_count]
    arrivals = scratch[3 * view_count : 4 * view_count]
    (
        keys, key_by_channel_ref, key_by_row_ref, warp_ref, species_out_ref, frame_ref,
        slab_send, slab_recv, tile_send, tile_recv, key_send, key_recv, local_sem,
    ) = scratch[4 * view_count : 4 * view_count + 13]
    advance_scratch = scratch[4 * view_count + 13 :]
    depth_cells, rows, width = shifted.shape[0], shifted.shape[3], shifted.shape[4]
    me_d, me_r, me_c = lax.axis_index("depth"), lax.axis_index("row"), lax.axis_index("col")

    def slab_of(step):
        return lax.rem(me_d + step, depth_devices)

    def tile_of(step):
        return lax.rem(me_c + step, tiles)

    barrier = pltpu.get_barrier_semaphore()
    for step in range(1, depth_devices):
        pl.semaphore_signal(barrier, inc=1, device_id=(slab_of(step), me_r, me_c), device_id_type=MESH)
    for step in range(1, tiles):
        pl.semaphore_signal(barrier, inc=1, device_id=(me_d, me_r, tile_of(step)), device_id_type=MESH)

    row_steps = sorted({1, row_devices - 1})
    for step in row_steps:
        row_peer = lax.rem(me_r + step, row_devices)
        pl.semaphore_signal(barrier, inc=1, device_id=(me_d, row_peer, me_c), device_id_type=MESH)
    warp_copy = pltpu.make_async_copy(
        warp_hbm.at[pl.ds(me_d * view_count, view_count)], warp_ref, local_sem.at[0]
    )
    warp_copy.start()
    pixels = 4 * rows
    earlier = lax.broadcasted_iota(jnp.int32, (pixels, pixels), 0)
    later = lax.broadcasted_iota(jnp.int32, (pixels, pixels), 1)
    line = lax.broadcasted_iota(jnp.int32, (rows, pixels), 0)
    spot = lax.broadcasted_iota(jnp.int32, (rows, pixels), 1)

    def spread(table, chosen):
        return jnp.dot(
            table.astype(jnp.float32).astype(jnp.bfloat16),
            jnp.where(chosen, 1.0, 0.0).astype(jnp.bfloat16),
            preferred_element_type=jnp.float32,
        ).astype(jnp.int32)

    for target, chosen, same in (
        (key_by_channel_ref, spot % rows == line, earlier // rows == later // rows),
        (key_by_row_ref, spot // 4 == line, earlier % 4 == later % 4),
    ):
        owners = spread(owner_ref[...], chosen)
        for number in range(view_count):
            owner = owners[number : number + 1, :]
            column = jnp.sum(jnp.where(earlier == later, owner, 0), axis=1, keepdims=True)
            before = (column == owner) & same & (earlier < later)
            rank = jnp.sum(jnp.where(before, 1, 0), axis=0, keepdims=True)
            target[number : number + 1, :] = owner * capacity + rank
    pl.semaphore_wait(barrier, depth_devices - 1 + tiles - 1 + len(row_steps))

    key_copies = []
    for step in range(1, tiles):
        copy = pltpu.make_async_remote_copy(
            src_ref=key_by_row_ref, dst_ref=keys.at[me_c],
            send_sem=key_send.at[step], recv_sem=key_recv.at[step],
            device_id=(me_d, me_r, tile_of(step)), device_id_type=MESH,
        )
        copy.start()
        key_copies.append(copy)
    keys[me_c] = key_by_row_ref[...]
    advance(
        depth_devices, row_devices, tiles, rim_width,
        species_ref, diffusivity_ref, rate_ref, species_out_ref, shifted, local_sem, *advance_scratch,
    )
    species_copy = pltpu.make_async_copy(species_out_ref, species_hbm, local_sem.at[1])
    species_copy.start()

    def render(view, out_ref):
        weights = [
            [weight_ref[2 * c + f, view] * (0.5 if c < 3 else 1.0) for f in range(2)] for c in range(4)
        ]
        biases = [bias_ref[c, view] * (0.5 if c < 3 else 1.0) for c in range(4)]
        shear = shear_ref[view]

        def cells(cell, state):
            red, green, blue, through = state
            at = start_ref[view, cell]
            place = (me_d * depth_cells + cell).astype(jnp.float32) + 0.5 - 0.5 * depth_cells * depth_devices
            fraction = shear * place - (at - rim_width).astype(jnp.float32)
            s0 = shifted[cell, at, 0] + fraction * shifted[cell, at, 1]
            s1 = shifted[cell, at, 2] + fraction * shifted[cell, at, 3]
            logits = [weights[c][0] * s0 + weights[c][1] * s1 + biases[c] for c in range(4)]
            fading = jnp.exp(-RAY_STEP * jnp.log(1.0 + jnp.exp(logits[3])))
            later = through * fading
            share = through - later
            return (
                red + share * jnp.tanh(logits[0]),
                green + share * jnp.tanh(logits[1]),
                blue + share * jnp.tanh(logits[2]),
                later,
            )

        zero = jnp.zeros((rows, width), jnp.float32)
        red, green, blue, through = lax.fori_loop(
            0, depth_cells, cells, (zero, zero, zero, zero + 1.0), unroll=4
        )
        opacity = 1.0 - through
        for channel, value in enumerate((red, green, blue, opacity)):
            value = value if channel == 3 else 0.5 * (value + opacity)
            root = jnp.sqrt(jnp.sqrt(jnp.clip(value, 0.0, 1.0)))
            out_ref[channel] = ((root * 65535.0 + 0.5).astype(jnp.int32) - 32768).astype(jnp.int16)

    slots = 4 * capacity

    def render_group(number):
        copies = []
        for step in list(range(1, depth_devices)) + [0]:
            view = slab_of(step) * view_count + number
            if step == 0:
                render(view, stacks[number].at[me_d])
            else:
                render(view, images[number].at[step])
                copy = pltpu.make_async_remote_copy(
                    src_ref=images[number].at[step], dst_ref=stacks[number].at[me_d],
                    send_sem=slab_send.at[number, step], recv_sem=slab_recv.at[number, step],
                    device_id=(slab_of(step), me_r, me_c), device_id_type=MESH,
                )
                copy.start()
                copies.append(copy)
        return copies

    def composite(number):
        view = me_d * view_count + number
        stack = stacks[number]

        def slab_at(position):
            code = stack[order_ref[position, view]].astype(jnp.int32)
            root = (code + 32768).astype(jnp.float32) * (1.0 / 65535.0)
            root = root * root
            return root * root

        result = slab_at(0)
        for position in range(1, depth_devices):
            result = result + (1.0 - result[3:4]) * slab_at(position)
        lane = lax.broadcasted_iota(jnp.int32, (rows, width), 1)
        at = lax.broadcasted_iota(jnp.int32, (rows, rows), 1)
        at = at == lax.broadcasted_iota(jnp.int32, (rows, rows), 0)
        length = length_ref[number : number + 1, :]
        keep = lane < jnp.sum(jnp.where(at, length, 0), axis=1, keepdims=True)
        picture = jnp.where(keep[None], result, 0.0).reshape(4 * rows, width).astype(jnp.bfloat16)
        line = lax.broadcasted_iota(jnp.int32, (tiles * slots, 4 * rows), 0)
        pixel = lax.broadcasted_iota(jnp.int32, (tiles * slots, 4 * rows), 1)
        wanted = (line // slots) * capacity + line % capacity
        key = key_by_channel_ref[number : number + 1, :]
        chosen = (wanted == key) & ((line // capacity) % 4 == pixel // rows)
        packed = jnp.dot(
            jnp.where(chosen, 1.0, 0.0).astype(jnp.bfloat16), picture, preferred_element_type=jnp.float32
        ).astype(jnp.bfloat16)
        packs[number][...] = packed.reshape(tiles, slots, width)
        arrivals[number][me_c] = packs[number][me_c]
        copies = []
        for step in range(1, tiles):
            copy = pltpu.make_async_remote_copy(
                src_ref=packs[number].at[tile_of(step)], dst_ref=arrivals[number].at[me_c],
                send_sem=tile_send.at[number, step], recv_sem=tile_recv.at[number, step],
                device_id=(me_d, me_r, tile_of(step)), device_id_type=MESH,
            )
            copy.start()
            copies.append(copy)
        return copies

    def warp(number):
        line = lax.broadcasted_iota(jnp.int32, (slots, 4 * rows), 0)
        pixel = lax.broadcasted_iota(jnp.int32, (slots, 4 * rows), 1)
        wanted = me_c * capacity + line % capacity
        same = line // capacity == pixel % 4
        places = [
            jnp.where((wanted == keys[tile, number : number + 1, :]) & same, 1.0, 0.0).astype(jnp.bfloat16)
            for tile in range(tiles)
        ]
        gathered = lax.dot_general(
            jnp.concatenate(places, axis=0),
            arrivals[number][...].reshape(tiles * slots, width),
            (((0,), (0,)), ((), ())),
            preferred_element_type=jnp.float32,
        )
        high = gathered.astype(jnp.bfloat16)
        low = (gathered - high.astype(jnp.float32)).astype(jnp.bfloat16)
        matrix = warp_ref[number]
        frame_ref[number] = jnp.dot(high, matrix, preferred_element_type=jnp.float32) + jnp.dot(
            low, matrix, preferred_element_type=jnp.float32
        )

    slab_copies, tile_copies, frame_copies = [], [], []
    for number in range(view_count):
        slab_copies.append(render_group(number))
        if number > 0:
            for copy in slab_copies[number - 1]:
                copy.wait()
            tile_copies.append(composite(number - 1))
    for copy in slab_copies[-1]:
        copy.wait()
    tile_copies.append(composite(view_count - 1))
    for copy in key_copies:
        copy.wait()
    for number in range(view_count):
        for copy in tile_copies[number]:
            copy.wait()
        if number == 0:
            warp_copy.wait()
        warp(number)
        copy = pltpu.make_async_copy(frame_ref.at[number], frame_hbm.at[number], local_sem.at[6 + number])
        copy.start()
        frame_copies.append(copy)
    for copy in [species_copy] + frame_copies:
        copy.wait()


def body(
    species, diffusivity, reaction_rate, shear_rate, colour_weight, colour_bias,
    slab_order, lengths, owners, warp_matrix,
):
    depth_cells, rows, width = species.shape[1:]
    depth_devices = lax.axis_size("depth")
    tiles = lax.axis_size("col")
    depth_total = depth_cells * depth_devices
    rim_width = (4 * depth_total + 99) // 100
    row_devices = lax.axis_size("row")
    planes, tall = depth_cells + 2 * LAYERS, rows + 8
    views = shear_rate.shape[0]
    view_count = views // depth_devices
    capacity = 2 * rows // tiles
    cell_at = lax.axis_index("depth") * depth_cells + jnp.arange(depth_cells, dtype=jnp.int32)
    offset = shear_rate[:, None] * (cell_at.astype(jnp.float32) + 0.5 - 0.5 * depth_total)
    floor_part = jnp.floor(offset)
    start = jnp.clip(floor_part.astype(jnp.int32) + rim_width, 0, 2 * rim_width - 1)
    slots = 4 * capacity
    vmem = pl.BlockSpec(memory_space=pltpu.VMEM)
    hbm = pl.BlockSpec(memory_space=pltpu.HBM)
    smem = pl.BlockSpec(memory_space=pltpu.SMEM)
    species_out, frame = pl.pallas_call(
        functools.partial(march_kernel, depth_devices, row_devices, tiles, capacity, rim_width),
        out_shape=(
            jax.ShapeDtypeStruct(species.shape, jnp.float32),
            jax.ShapeDtypeStruct((view_count, 4 * rows, width), jnp.float32),
        ),
        in_specs=[smem] * 5 + [hbm] * 3 + [vmem, vmem, hbm],
        out_specs=(hbm, hbm),
        scratch_shapes=[pltpu.VMEM((depth_cells, 2 * rim_width, 4, rows, width), jnp.float32)]
        + [pltpu.VMEM((depth_devices, 4, rows, width), jnp.int16)] * view_count
        + [pltpu.VMEM((depth_devices, 4, rows, width), jnp.int16)] * view_count
        + [pltpu.VMEM((tiles, slots, width), jnp.bfloat16)] * view_count
        + [pltpu.VMEM((tiles, slots, width), jnp.bfloat16)] * view_count
        + [
            pltpu.VMEM((tiles, view_count, 4 * rows), jnp.int32),
            pltpu.VMEM((view_count, 4 * rows), jnp.int32),
            pltpu.VMEM((view_count, 4 * rows), jnp.int32),
            pltpu.VMEM((view_count, *warp_matrix.shape[1:]), warp_matrix.dtype),
            pltpu.VMEM(species.shape, jnp.float32),
            pltpu.VMEM((view_count, 4 * rows, width), jnp.float32),
            pltpu.SemaphoreType.DMA((view_count, depth_devices)),
            pltpu.SemaphoreType.DMA((view_count, depth_devices)),
            pltpu.SemaphoreType.DMA((view_count, tiles)),
            pltpu.SemaphoreType.DMA((view_count, tiles)),
            pltpu.SemaphoreType.DMA((tiles,)),
            pltpu.SemaphoreType.DMA((tiles,)),
            pltpu.SemaphoreType.DMA((6 + view_count,)),
        ]
        + [
            pltpu.VMEM((4, planes, tall, 2 * width), jnp.float32),
            pltpu.VMEM((2, planes, tall, 2 * width), jnp.float32),
            pltpu.VMEM((2, planes, tall, 2 * width), jnp.float32),
            pltpu.VMEM((tall, 2 * width), jnp.float32),
            pltpu.VMEM((2, 4, depth_cells, 8, width), jnp.float32),
            pltpu.VMEM((2, 4, tall, width), jnp.float32),
            pltpu.VMEM((2, 4, tall, width), jnp.float32),
            pltpu.VMEM((2, 6, 2 * tall, width), jnp.bfloat16),
            pltpu.VMEM((2, 6, 2 * tall, width), jnp.bfloat16),
            pltpu.SemaphoreType.DMA((10,)),
            pltpu.SemaphoreType.DMA((10,)),
        ],
        compiler_params=pltpu.CompilerParams(
            collective_id=1, has_side_effects=True, vmem_limit_bytes=60 * 1024 * 1024
        ),
    )(
        shear_rate, colour_weight.transpose(1, 2, 0).reshape(8, views), colour_bias.T, start, slab_order.T,
        species, diffusivity, reaction_rate, owners[:, 0, :, 0], lengths[:, 0], warp_matrix,
    )
    return (species_out, frame.reshape(view_count, rows, 4, width))


def solution(mesh):
    in_specs = (
        P(None, "depth", "row", "col"),
        P("depth", "row", "col"),
        P("depth", "row", "col"),
        P(),
        P(),
        P(),
        P(),
        P("depth", "col", "row"),
        P("depth", "col", "row", None),
        P(),
    )
    out_specs = (P(None, "depth", "row", "col"), P("depth", "row", None, "col"))
    return jax.shard_map(body, mesh=mesh, in_specs=in_specs, out_specs=out_specs, check_vma=False)
```

```python
import functools

import jax
import jax.numpy as jnp
from jax import lax
from jax.experimental import pallas as pl
from jax.experimental.pallas import tpu as pltpu
from jax.sharding import PartitionSpec as P

TIME_STEP = 0.1
RAY_STEP = 0.02
VEL_DEPTH = 0.3
VEL_ROW = 0.2
VEL_COL = 0.4


MESH = pl.DeviceIdType.MESH

LAYERS = 3


def advance(
    depth_devices, row_devices, tiles, rim_width,
    species_ref, diffusivity_ref, rate_ref, species_out_ref, shifted, local_sem,
    deep, first_ref, second_ref, step_ref, row_got, packs, got, stage_out, stage_in, send_sem, recv_sem,
):
    me_d, me_r, me_c = lax.axis_index("depth"), lax.axis_index("row"), lax.axis_index("col")
    depth_cells, rows, width = species_ref.shape[1:]
    tall, wide = rows + 8, 2 * width
    edge = LAYERS + rim_width
    last = LAYERS + depth_cells

    def link(number, src, dst, device):
        return pltpu.make_async_remote_copy(
            src_ref=src, dst_ref=dst, send_sem=send_sem.at[number], recv_sem=recv_sem.at[number],
            device_id=device, device_id_type=MESH,
        )

    def begin(place, count, down, up):
        @pl.when(place > 0)
        def _():
            for copy in down:
                copy.start()

        @pl.when(place < count - 1)
        def _():
            for copy in up:
                copy.start()

    def finish(place, count, down, up, below, above):
        @pl.when(place > 0)
        def _():
            for copy in down:
                copy.wait_send()
            for copy in up:
                copy.wait_recv()

        @pl.when(place < count - 1)
        def _():
            for copy in up:
                copy.wait_send()
            for copy in down:
                copy.wait_recv()

        @pl.when(place == 0)
        def _():
            below[...] = jnp.zeros(below.shape, below.dtype)

        @pl.when(place == count - 1)
        def _():
            above[...] = jnp.zeros(above.shape, above.dtype)

    row_down = (me_d, lax.rem(me_r + row_devices - 1, row_devices), me_c)
    row_up = (me_d, lax.rem(me_r + 1, row_devices), me_c)
    col_down = (me_d, me_r, lax.rem(me_c + tiles - 1, tiles))
    col_up = (me_d, me_r, lax.rem(me_c + 1, tiles))
    depth_down = (lax.rem(me_d + depth_devices - 1, depth_devices), me_r, me_c)
    depth_up = (lax.rem(me_d + 1, depth_devices), me_r, me_c)

    low, high = pl.ds(0, 8), pl.ds(rows - 8, 8)
    down = [
        link(0, species_ref.at[:, :, low], row_got.at[1, pl.ds(0, 2)], row_down),
        link(1, diffusivity_ref.at[:, low], row_got.at[1, 2], row_down),
        link(2, rate_ref.at[:, low], row_got.at[1, 3], row_down),
    ]
    up = [
        link(3, species_ref.at[:, :, high], row_got.at[0, pl.ds(0, 2)], row_up),
        link(4, diffusivity_ref.at[:, high], row_got.at[0, 2], row_up),
        link(5, rate_ref.at[:, high], row_got.at[0, 3], row_up),
    ]
    begin(me_r, row_devices, down, up)

    own = (pl.ds(LAYERS, depth_cells), pl.ds(0, rows), pl.ds(0, width))
    sources = (species_ref.at[0], species_ref.at[1], diffusivity_ref, rate_ref)
    local = [
        pltpu.make_async_copy(source, deep.at[(field, *own)], local_sem.at[2 + field])
        for field, source in enumerate(sources)
    ]
    for copy in local:
        copy.start()
    row_at = lax.broadcasted_iota(jnp.int32, (tall, wide), 0)
    row_at = me_r * rows + jnp.where(row_at < rows + 4, row_at, row_at - tall)
    col_at = lax.broadcasted_iota(jnp.int32, (tall, wide), 1)
    col_at = me_c * width + jnp.where(col_at < width + width // 2, col_at, col_at - wide)
    inside = (row_at >= 0) & (row_at < rows * row_devices) & (col_at >= 0) & (col_at < width * tiles)
    step_ref[...] = jnp.where(inside, TIME_STEP, 0.0)
    finish(me_r, row_devices, down, up, row_got.at[0], row_got.at[1])

    for copy in local:
        copy.wait()
    near = lax.broadcasted_iota(jnp.int32, (8, width), 0) < 4

    def place_rows(cell, carry):
        for field in range(4):
            deep[field, LAYERS + cell, pl.ds(rows, 8), pl.ds(0, width)] = jnp.where(
                near, row_got[1, field, cell], row_got[0, field, cell]
            )
        return carry

    lax.fori_loop(0, depth_cells, place_rows, 0)

    lower = [(f, LAYERS + k, last + k) for f in range(2) for k in range(3)]
    lower += [(f, LAYERS + k, last + k) for f in range(2, 4) for k in range(2)]
    upper = [(f, last - 3 + k, k) for f in range(2) for k in range(3)]
    upper += [(f, last - 3 + k, k) for f in range(2, 4) for k in range(1, 3)]
    for way, items in enumerate((lower, upper)):
        for pair in range(len(items) // 2):
            planes = [deep[f, here, :, pl.ds(0, width)] for f, here, _ in items[2 * pair : 2 * pair + 2]]
            stage_out[way, pair] = jnp.concatenate(planes, axis=0).astype(jnp.bfloat16)
    body, rest = pl.ds(0, len(lower) // 2), pl.ds(len(lower) // 2, 1)
    deep_down = [link(8, stage_out.at[0, body], stage_in.at[1, body], depth_down)]
    deep_up = [link(9, stage_out.at[1, body], stage_in.at[0, body], depth_up)]
    begin(me_d, depth_devices, deep_down, deep_up)

    lane = lax.broadcasted_iota(jnp.int32, (tall, width), 1)

    def turned(array, shift):
        shift = shift % width
        return array if shift == 0 else pltpu.roll(array, shift, 1)

    def pack_columns(field, carry):
        left = jnp.zeros((tall, width), jnp.float32)
        right = left
        for cell in range(depth_cells):
            plane = deep[field, LAYERS + cell, :, pl.ds(0, width)]
            here = (lane >= edge * cell) & (lane < edge * (cell + 1))
            left = jnp.where(here, turned(plane, edge * cell), left)
            right = jnp.where(here, turned(plane, edge * (cell + 1)), right)
        packs[0, field] = left
        packs[1, field] = right
        return carry

    lax.fori_loop(0, 4, pack_columns, 0)
    down = [link(6, packs.at[0], got.at[1], col_down)]
    up = [link(7, packs.at[1], got.at[0], col_up)]
    begin(me_c, tiles, down, up)
    finish(me_c, tiles, down, up, got.at[0], got.at[1])

    def side_tile(below, below_at, above, above_at):
        return jnp.where(
            lane < edge,
            turned(above, -above_at),
            jnp.where(lane >= width - edge, turned(below, width - edge - below_at), 0.0),
        )

    span = 3 * edge

    def corner_at(field, side):
        return (field % 2) * (width // 2) + side * (width // 4)

    for way, (items, start) in enumerate(((lower, 0), (upper, edge * (depth_cells - 3)))):
        corners = []
        for half in range(2):
            tile = jnp.zeros((tall, width), jnp.float32)
            for field in (2 * half, 2 * half + 1):
                for side in range(2):
                    at = corner_at(field, side)
                    here = (lane >= at) & (lane < at + span)
                    tile = jnp.where(here, turned(got[side, field], at - start), tile)
            corners.append(tile)
        stage_out[way, len(items) // 2] = jnp.concatenate(corners, axis=0).astype(jnp.bfloat16)
    down = [link(10, stage_out.at[0, rest], stage_in.at[1, rest], depth_down)]
    up = [link(11, stage_out.at[1, rest], stage_in.at[0, rest], depth_up)]
    begin(me_d, depth_devices, down, up)

    def place_sides(field, carry):
        for cell in range(depth_cells):
            deep[field, LAYERS + cell, :, pl.ds(width, width)] = side_tile(
                got[0, field], edge * cell, got[1, field], edge * cell
            )
        return carry

    lax.fori_loop(0, 4, place_sides, 0)

    def rates_of(source, plane):
        time_step = step_ref[...]
        at = me_d * depth_cells + plane - LAYERS
        time_step = time_step * jnp.where((at >= 0) & (at < depth_cells * depth_devices), 1.0, 0.0)
        fuel, heat = source[0, plane], source[1, plane]
        squared = heat * heat
        burned = deep[3, plane] * fuel * squared / (1.0 + squared)
        spread = deep[2, plane]
        changes = []
        for field, centre in ((0, fuel), (1, heat)):
            below_depth, above_depth = source[field, plane - 1], source[field, plane + 1]
            below_row, above_row = pltpu.roll(centre, 1, 0), pltpu.roll(centre, tall - 1, 0)
            below_col, above_col = pltpu.roll(centre, 1, 1), pltpu.roll(centre, wide - 1, 1)
            laplace = (
                below_depth + above_depth + below_row + above_row + below_col + above_col - 6.0 * centre
            )
            carried = (
                VEL_DEPTH * below_depth + VEL_ROW * below_row + VEL_COL * below_col
                - (VEL_DEPTH + VEL_ROW + VEL_COL) * centre
            )
            total = spread * laplace + carried
            total = total - burned if field == 0 else total + burned
            changes.append(centre + time_step * total)
        return changes

    def first_stage(plane):
        for field, value in enumerate(rates_of(deep, plane)):
            first_ref[field, plane] = value

    def second_stage(plane):
        for field, value in enumerate(rates_of(first_ref, plane)):
            second_ref[field, plane] = 0.75 * deep[field, plane] + 0.25 * value

    def third_stage(plane):
        cell = plane - LAYERS
        for field, value in enumerate(rates_of(second_ref, plane)):
            final = deep[field, plane] * (1.0 / 3.0) + (2.0 / 3.0) * value
            final = final[:rows]
            species_out_ref[field, cell] = final[:, :width]
            earlier = pltpu.roll(final, rim_width, 1)[:, :width]
            for shift in range(2 * rim_width):
                turn = (rim_width - shift - 1) % wide
                later = (final if turn == 0 else pltpu.roll(final, turn, 1))[:, :width]
                shifted[cell, shift, 2 * field] = earlier
                shifted[cell, shift, 2 * field + 1] = later - earlier
                earlier = later

    def inner(stage, begin_at, end_at):
        def one(plane, carry):
            stage(plane)
            return carry

        lax.fori_loop(begin_at, end_at, one, 0)

    def outer(stage, begin_at, gap):
        def one(number, carry):
            stage(begin_at + number + (number // 3) * gap)
            return carry

        lax.fori_loop(0, 6, one, 0)

    inner(first_stage, LAYERS + 1, last - 1)
    inner(second_stage, LAYERS + 2, last - 2)
    inner(third_stage, LAYERS + 3, last - 3)
    finish(me_d, depth_devices, deep_down + down, deep_up + up, stage_in.at[0], stage_in.at[1])
    for way, (items, place) in enumerate(((upper, 0), (lower, last))):
        pairs = len(items) // 2
        corners = stage_in[way, pairs].astype(jnp.float32)
        for pair in range(pairs):
            both = stage_in[way, pair].astype(jnp.float32)
            for half in range(2):
                field, _, there = items[2 * pair + half]
                deep[field, there, :, pl.ds(0, width)] = both[half * tall : (half + 1) * tall]
                tile = corners[field // 2 * tall : (field // 2 + 1) * tall]
                layer = edge * (there - place)
                deep[field, there, :, pl.ds(width, width)] = side_tile(
                    tile, corner_at(field, 0) + layer, tile, corner_at(field, 1) + layer
                )
    outer(first_stage, 1, depth_cells - 2)
    outer(second_stage, 2, depth_cells - 4)
    outer(third_stage, 3, depth_cells - 6)


def march_kernel(
    depth_devices, row_devices, tiles, capacity, rim_width,
    shear_ref, weight_ref, bias_ref, start_ref, order_ref,
    species_ref, diffusivity_ref, rate_ref, owner_ref, length_ref, warp_hbm,
    species_hbm, frame_hbm,
    shifted, *scratch,
):
    view_count = frame_hbm.shape[0]
    stacks = scratch[:view_count]
    images = scratch[view_count : 2 * view_count]
    packs = scratch[2 * view_count : 3 * view_count]
    arrivals = scratch[3 * view_count : 4 * view_count]
    (
        keys, key_by_channel_ref, key_by_row_ref, warp_ref, species_out_ref, frame_ref,
        slab_send, slab_recv, tile_send, tile_recv, key_send, key_recv, local_sem,
    ) = scratch[4 * view_count : 4 * view_count + 13]
    advance_scratch = scratch[4 * view_count + 13 :]
    depth_cells, rows, width = shifted.shape[0], shifted.shape[3], shifted.shape[4]
    me_d, me_r, me_c = lax.axis_index("depth"), lax.axis_index("row"), lax.axis_index("col")

    def slab_of(step):
        return lax.rem(me_d + step, depth_devices)

    def tile_of(step):
        return lax.rem(me_c + step, tiles)

    barrier = pltpu.get_barrier_semaphore()
    for step in range(1, depth_devices):
        pl.semaphore_signal(barrier, inc=1, device_id=(slab_of(step), me_r, me_c), device_id_type=MESH)
    for step in range(1, tiles):
        pl.semaphore_signal(barrier, inc=1, device_id=(me_d, me_r, tile_of(step)), device_id_type=MESH)

    row_steps = sorted({1, row_devices - 1})
    for step in row_steps:
        row_peer = lax.rem(me_r + step, row_devices)
        pl.semaphore_signal(barrier, inc=1, device_id=(me_d, row_peer, me_c), device_id_type=MESH)
    warp_copy = pltpu.make_async_copy(
        warp_hbm.at[pl.ds(me_d * view_count, view_count)], warp_ref, local_sem.at[0]
    )
    warp_copy.start()
    pixels = 4 * rows
    earlier = lax.broadcasted_iota(jnp.int32, (pixels, pixels), 0)
    later = lax.broadcasted_iota(jnp.int32, (pixels, pixels), 1)
    line = lax.broadcasted_iota(jnp.int32, (rows, pixels), 0)
    spot = lax.broadcasted_iota(jnp.int32, (rows, pixels), 1)

    def spread(table, chosen):
        return jnp.dot(
            table.astype(jnp.float32).astype(jnp.bfloat16),
            jnp.where(chosen, 1.0, 0.0).astype(jnp.bfloat16),
            preferred_element_type=jnp.float32,
        ).astype(jnp.int32)

    for target, chosen, same in (
        (key_by_channel_ref, spot % rows == line, earlier // rows == later // rows),
        (key_by_row_ref, spot // 4 == line, earlier % 4 == later % 4),
    ):
        owners = spread(owner_ref[...], chosen)
        for number in range(view_count):
            owner = owners[number : number + 1, :]
            column = jnp.sum(jnp.where(earlier == later, owner, 0), axis=1, keepdims=True)
            before = (column == owner) & same & (earlier < later)
            rank = jnp.sum(jnp.where(before, 1, 0), axis=0, keepdims=True)
            target[number : number + 1, :] = owner * capacity + rank
    pl.semaphore_wait(barrier, depth_devices - 1 + tiles - 1 + len(row_steps))

    key_copies = []
    for step in range(1, tiles):
        copy = pltpu.make_async_remote_copy(
            src_ref=key_by_row_ref, dst_ref=keys.at[me_c],
            send_sem=key_send.at[step], recv_sem=key_recv.at[step],
            device_id=(me_d, me_r, tile_of(step)), device_id_type=MESH,
        )
        copy.start()
        key_copies.append(copy)
    keys[me_c] = key_by_row_ref[...]
    advance(
        depth_devices, row_devices, tiles, rim_width,
        species_ref, diffusivity_ref, rate_ref, species_out_ref, shifted, local_sem, *advance_scratch,
    )
    species_copy = pltpu.make_async_copy(species_out_ref, species_hbm, local_sem.at[1])
    species_copy.start()

    def render(view, out_ref):
        weights = [
            [weight_ref[2 * c + f, view] * (0.5 if c < 3 else 1.0) for f in range(2)] for c in range(4)
        ]
        biases = [bias_ref[c, view] * (0.5 if c < 3 else 1.0) for c in range(4)]
        shear = shear_ref[view]

        def cells(cell, state):
            red, green, blue, through = state
            at = start_ref[view, cell]
            place = (me_d * depth_cells + cell).astype(jnp.float32) + 0.5 - 0.5 * depth_cells * depth_devices
            fraction = shear * place - (at - rim_width).astype(jnp.float32)
            s0 = shifted[cell, at, 0] + fraction * shifted[cell, at, 1]
            s1 = shifted[cell, at, 2] + fraction * shifted[cell, at, 3]
            logits = [weights[c][0] * s0 + weights[c][1] * s1 + biases[c] for c in range(4)]
            fading = jnp.exp(-RAY_STEP * jnp.log(1.0 + jnp.exp(logits[3])))
            later = through * fading
            share = through - later
            return (
                red + share * jnp.tanh(logits[0]),
                green + share * jnp.tanh(logits[1]),
                blue + share * jnp.tanh(logits[2]),
                later,
            )

        zero = jnp.zeros((rows, width), jnp.float32)
        red, green, blue, through = lax.fori_loop(
            0, depth_cells, cells, (zero, zero, zero, zero + 1.0), unroll=8
        )
        opacity = 1.0 - through
        for channel, value in enumerate((red, green, blue, opacity)):
            value = value if channel == 3 else 0.5 * (value + opacity)
            root = jnp.sqrt(jnp.sqrt(jnp.clip(value, 0.0, 1.0)))
            out_ref[channel] = ((root * 65535.0 + 0.5).astype(jnp.int32) - 32768).astype(jnp.int16)

    slots = 4 * capacity

    def render_group(number):
        copies = []
        for step in list(range(1, depth_devices)) + [0]:
            view = slab_of(step) * view_count + number
            if step == 0:
                render(view, stacks[number].at[me_d])
            else:
                render(view, images[number].at[step])
                copy = pltpu.make_async_remote_copy(
                    src_ref=images[number].at[step], dst_ref=stacks[number].at[me_d],
                    send_sem=slab_send.at[number, step], recv_sem=slab_recv.at[number, step],
                    device_id=(slab_of(step), me_r, me_c), device_id_type=MESH,
                )
                copy.start()
                copies.append(copy)
        return copies

    def composite(number):
        view = me_d * view_count + number
        stack = stacks[number]

        def slab_at(position):
            code = stack[order_ref[position, view]].astype(jnp.int32)
            root = (code + 32768).astype(jnp.float32) * (1.0 / 65535.0)
            root = root * root
            return root * root

        result = slab_at(0)
        for position in range(1, depth_devices):
            result = result + (1.0 - result[3:4]) * slab_at(position)
        lane = lax.broadcasted_iota(jnp.int32, (rows, width), 1)
        at = lax.broadcasted_iota(jnp.int32, (rows, rows), 1)
        at = at == lax.broadcasted_iota(jnp.int32, (rows, rows), 0)
        length = length_ref[number : number + 1, :]
        keep = lane < jnp.sum(jnp.where(at, length, 0), axis=1, keepdims=True)
        picture = jnp.where(keep[None], result, 0.0).reshape(4 * rows, width).astype(jnp.bfloat16)
        line = lax.broadcasted_iota(jnp.int32, (tiles * slots, 4 * rows), 0)
        pixel = lax.broadcasted_iota(jnp.int32, (tiles * slots, 4 * rows), 1)
        wanted = (line // slots) * capacity + line % capacity
        key = key_by_channel_ref[number : number + 1, :]
        chosen = (wanted == key) & ((line // capacity) % 4 == pixel // rows)
        packed = jnp.dot(
            jnp.where(chosen, 1.0, 0.0).astype(jnp.bfloat16), picture, preferred_element_type=jnp.float32
        ).astype(jnp.bfloat16)
        packs[number][...] = packed.reshape(tiles, slots, width)
        arrivals[number][me_c] = packs[number][me_c]
        copies = []
        for step in range(1, tiles):
            copy = pltpu.make_async_remote_copy(
                src_ref=packs[number].at[tile_of(step)], dst_ref=arrivals[number].at[me_c],
                send_sem=tile_send.at[number, step], recv_sem=tile_recv.at[number, step],
                device_id=(me_d, me_r, tile_of(step)), device_id_type=MESH,
            )
            copy.start()
            copies.append(copy)
        return copies

    def warp(number):
        line = lax.broadcasted_iota(jnp.int32, (slots, 4 * rows), 0)
        pixel = lax.broadcasted_iota(jnp.int32, (slots, 4 * rows), 1)
        wanted = me_c * capacity + line % capacity
        same = line // capacity == pixel % 4
        places = [
            jnp.where((wanted == keys[tile, number : number + 1, :]) & same, 1.0, 0.0).astype(jnp.bfloat16)
            for tile in range(tiles)
        ]
        gathered = lax.dot_general(
            jnp.concatenate(places, axis=0),
            arrivals[number][...].reshape(tiles * slots, width),
            (((0,), (0,)), ((), ())),
            preferred_element_type=jnp.float32,
        )
        high = gathered.astype(jnp.bfloat16)
        low = (gathered - high.astype(jnp.float32)).astype(jnp.bfloat16)
        matrix = warp_ref[number]
        frame_ref[number] = jnp.dot(high, matrix, preferred_element_type=jnp.float32) + jnp.dot(
            low, matrix, preferred_element_type=jnp.float32
        )

    slab_copies, tile_copies, frame_copies = [], [], []
    for number in range(view_count):
        slab_copies.append(render_group(number))
        if number > 0:
            for copy in slab_copies[number - 1]:
                copy.wait()
            tile_copies.append(composite(number - 1))
    for copy in slab_copies[-1]:
        copy.wait()
    tile_copies.append(composite(view_count - 1))
    for copy in key_copies:
        copy.wait()
    for number in range(view_count):
        for copy in tile_copies[number]:
            copy.wait()
        if number == 0:
            warp_copy.wait()
        warp(number)
        copy = pltpu.make_async_copy(frame_ref.at[number], frame_hbm.at[number], local_sem.at[6 + number])
        copy.start()
        frame_copies.append(copy)
    for copy in [species_copy] + frame_copies:
        copy.wait()


def body(
    species, diffusivity, reaction_rate, shear_rate, colour_weight, colour_bias,
    slab_order, lengths, owners, warp_matrix,
):
    depth_cells, rows, width = species.shape[1:]
    depth_devices = lax.axis_size("depth")
    tiles = lax.axis_size("col")
    depth_total = depth_cells * depth_devices
    rim_width = (4 * depth_total + 99) // 100
    row_devices = lax.axis_size("row")
    planes, tall = depth_cells + 2 * LAYERS, rows + 8
    views = shear_rate.shape[0]
    view_count = views // depth_devices
    capacity = 2 * rows // tiles
    cell_at = lax.axis_index("depth") * depth_cells + jnp.arange(depth_cells, dtype=jnp.int32)
    offset = shear_rate[:, None] * (cell_at.astype(jnp.float32) + 0.5 - 0.5 * depth_total)
    floor_part = jnp.floor(offset)
    start = jnp.clip(floor_part.astype(jnp.int32) + rim_width, 0, 2 * rim_width - 1)
    slots = 4 * capacity
    vmem = pl.BlockSpec(memory_space=pltpu.VMEM)
    hbm = pl.BlockSpec(memory_space=pltpu.HBM)
    smem = pl.BlockSpec(memory_space=pltpu.SMEM)
    species_out, frame = pl.pallas_call(
        functools.partial(march_kernel, depth_devices, row_devices, tiles, capacity, rim_width),
        out_shape=(
            jax.ShapeDtypeStruct(species.shape, jnp.float32),
            jax.ShapeDtypeStruct((view_count, 4 * rows, width), jnp.float32),
        ),
        in_specs=[smem] * 5 + [hbm] * 3 + [vmem, vmem, hbm],
        out_specs=(hbm, hbm),
        scratch_shapes=[pltpu.VMEM((depth_cells, 2 * rim_width, 4, rows, width), jnp.float32)]
        + [pltpu.VMEM((depth_devices, 4, rows, width), jnp.int16)] * view_count
        + [pltpu.VMEM((depth_devices, 4, rows, width), jnp.int16)] * view_count
        + [pltpu.VMEM((tiles, slots, width), jnp.bfloat16)] * view_count
        + [pltpu.VMEM((tiles, slots, width), jnp.bfloat16)] * view_count
        + [
            pltpu.VMEM((tiles, view_count, 4 * rows), jnp.int32),
            pltpu.VMEM((view_count, 4 * rows), jnp.int32),
            pltpu.VMEM((view_count, 4 * rows), jnp.int32),
            pltpu.VMEM((view_count, *warp_matrix.shape[1:]), warp_matrix.dtype),
            pltpu.VMEM(species.shape, jnp.float32),
            pltpu.VMEM((view_count, 4 * rows, width), jnp.float32),
            pltpu.SemaphoreType.DMA((view_count, depth_devices)),
            pltpu.SemaphoreType.DMA((view_count, depth_devices)),
            pltpu.SemaphoreType.DMA((view_count, tiles)),
            pltpu.SemaphoreType.DMA((view_count, tiles)),
            pltpu.SemaphoreType.DMA((tiles,)),
            pltpu.SemaphoreType.DMA((tiles,)),
            pltpu.SemaphoreType.DMA((6 + view_count,)),
        ]
        + [
            pltpu.VMEM((4, planes, tall, 2 * width), jnp.float32),
            pltpu.VMEM((2, planes, tall, 2 * width), jnp.float32),
            pltpu.VMEM((2, planes, tall, 2 * width), jnp.float32),
            pltpu.VMEM((tall, 2 * width), jnp.float32),
            pltpu.VMEM((2, 4, depth_cells, 8, width), jnp.float32),
            pltpu.VMEM((2, 4, tall, width), jnp.float32),
            pltpu.VMEM((2, 4, tall, width), jnp.float32),
            pltpu.VMEM((2, 6, 2 * tall, width), jnp.bfloat16),
            pltpu.VMEM((2, 6, 2 * tall, width), jnp.bfloat16),
            pltpu.SemaphoreType.DMA((12,)),
            pltpu.SemaphoreType.DMA((12,)),
        ],
        compiler_params=pltpu.CompilerParams(
            collective_id=1, has_side_effects=True, vmem_limit_bytes=60 * 1024 * 1024
        ),
    )(
        shear_rate, colour_weight.transpose(1, 2, 0).reshape(8, views), colour_bias.T, start, slab_order.T,
        species, diffusivity, reaction_rate, owners[:, 0, :, 0], lengths[:, 0], warp_matrix,
    )
    return (species_out, frame.reshape(view_count, rows, 4, width))


def solution(mesh):
    in_specs = (
        P(None, "depth", "row", "col"),
        P("depth", "row", "col"),
        P("depth", "row", "col"),
        P(),
        P(),
        P(),
        P(),
        P("depth", "col", "row"),
        P("depth", "col", "row", None),
        P(),
    )
    out_specs = (P(None, "depth", "row", "col"), P("depth", "row", None, "col"))
    return jax.shard_map(body, mesh=mesh, in_specs=in_specs, out_specs=out_specs, check_vma=False)
```
